256 devices in a mesh: row: 8 (over y, core), col: 8 (over z), level: 4 (over x).
Axes of the slice: x: 4, y: 4, z: 8, core: 2. Of those that a mesh axis runs over, the one named last changes fastest.
Arguments:
- pre_acts: bfloat16 [4, 2, 512, 64, 1024], P('level', None, 'row', None, 'col'), may hold values from -6 to 6
- pred_cot: bfloat16 [4, 512, 1024], P('level', 'row', 'col'), may hold values from -6 to 6
- occupancy: int32 [4, 512, 1024], P('level', 'row', 'col'), may hold values from 0 to 1
- conv_weights: bfloat16 [4, 2, 3, 3, 64, 64], P('level'), may hold values from -0.25 to 0.25
- coupling: bfloat16 [4, 2, 64], P('level'), may hold values from -3 to 3
- dilation: int32 [2], replicated, may hold values from 1 to 16, as said below
Outputs:
- attribution: bfloat16 [4, 512, 64, 1024], P('level', 'row', None, 'col')
The draws below stay inside these ranges and needn't reach their ends.
Inputs may be any that keep to these rules, and one draw needn't show every extreme that they name: Some layer has dilation 16.
All inputs are finite; a program needn't handle non-finite values.
Results may differ from the reference program's by a relative error of at most 0.02.
Values may be sent and summed in bfloat16 or wider, within the bound.
A program may use at most 64 MiB of HBM per device.

```python
import jax
import jax.numpy as jnp
from jax import lax

C = 64
LAYERS = 2
DMAX = 16
LEVELS = 4
NR = 512
NC = 1024


def draw_dilation(key, part):
    key = jax.random.fold_in(key, 11)
    first, second = jax.random.split(key)
    spacing = jax.random.randint(first, (LAYERS,), 1, DMAX + 1)
    chosen = jax.random.randint(second, (), 0, LAYERS)
    return jnp.where(jnp.arange(LAYERS) == chosen, DMAX, spacing).astype(jnp.int32)


def draw_occupancy(key, part):
    key = jax.random.fold_in(key, 23)
    first, second, third = jax.random.split(key, 3)
    rows_grid = jnp.arange(NR, dtype=jnp.int32)[None, :, None]
    cols_grid = jnp.arange(NC, dtype=jnp.int32)[None, None, :]
    band_width = jax.random.randint(first, (LEVELS, 1, 1), NC // 8, NC // 2 + 1)
    inside = jnp.abs(rows_grid * NC - cols_grid * NR) <= band_width * NR
    keep_rows = jax.random.randint(second, (LEVELS, NR, 1), 0, 10) > 0
    keep_cols = jax.random.randint(third, (LEVELS, 1, NC), 0, 10) > 0
    return (inside & keep_rows & keep_cols).astype(jnp.int32)


def shard_levels(stream_key, extent, cuts, least, high):
    factor_of = 1.0
    for dim, shards_of in cuts:
        heights = jax.random.uniform(jax.random.fold_in(jax.random.fold_in(stream_key, 6), dim), (shards_of,), jnp.float32, least / len(cuts), high / len(cuts))
        factor_of = factor_of * jnp.repeat(jnp.exp(heights), extent[dim] // shards_of).reshape((-1,) + (1,) * (len(extent) - 1 - dim))
    return factor_of


def noise(own_key, dims, width, limit, pieces=(), kind=jnp.bfloat16):
    gain = shard_levels(own_key, dims, pieces, -0.22, 0.18) if pieces else 1.0
    entries = jax.random.normal(own_key, dims, jnp.float32) * width * gain
    return jnp.minimum(jnp.maximum(entries, -limit), limit).astype(kind)


def setup_inputs(seed: int = 0) -> dict:
    key_list = jax.random.split(jax.random.key(seed), 7)
    pre_acts = noise(key_list[0], (LEVELS, LAYERS, NR, C, NC), 1.0, 6.0, ((0, 4), (2, 8), (4, 8)))
    pred_cot = noise(key_list[1], (LEVELS, NR, NC), 1.0, 6.0, ((0, 4), (1, 8), (2, 8)))
    occupancy = draw_occupancy(jax.random.fold_in(key_list[6], 71), 0)
    conv_weights = noise(key_list[3], (LEVELS, LAYERS, 3, 3, C, C), (9 * C) ** -0.5, 0.25, ((0, 4),))
    coupling = noise(key_list[4], (LEVELS, 2, C), 0.35, 3.0, ((0, 4),))
    dilation = draw_dilation(jax.random.fold_in(key_list[6], 71), 0)
    return dict(pre_acts=pre_acts, pred_cot=pred_cot, occupancy=occupancy, conv_weights=conv_weights, coupling=coupling, dilation=dilation)


def level_backward(layer_weights, head_row, pre_level, cot_level, incoming, dilation):
    total = cot_level.astype(jnp.float32) + incoming
    gradient = head_row.astype(jnp.float32)[None, :, None] * total[:, None, :]
    rows_here = gradient.shape[0]
    cols_here = gradient.shape[2]
    zero_index = jnp.zeros((), jnp.int32)
    for layer in reversed(range(LAYERS)):
        masked = jnp.where(pre_level[layer] > 0, gradient, 0.0).astype(jnp.bfloat16)
        padded = jnp.pad(masked, ((DMAX, DMAX), (0, 0), (DMAX, DMAX))).astype(jnp.float32)
        spacing = dilation[layer].astype(jnp.int32)
        summed = gradient
        for a in (-1, 0, 1):
            for b in (-1, 0, 1):
                start_row = (DMAX - a * spacing).astype(jnp.int32)
                start_col = (DMAX - b * spacing).astype(jnp.int32)
                portion = lax.dynamic_slice(padded, (start_row, zero_index, start_col), (rows_here, C, cols_here))
                kernel = layer_weights[layer, a + 1, b + 1].astype(jnp.float32)
                summed = summed + jnp.einsum('oc,row->rcw', kernel, portion)
        gradient = summed
    return gradient


def reference(pre_acts, pred_cot, occupancy, conv_weights, coupling, dilation):
    start_cot = jnp.where(occupancy > 0, pred_cot, jnp.zeros_like(pred_cot))
    incoming = jnp.zeros((NR, NC), jnp.float32)
    results = [None] * LEVELS
    for level_index in reversed(range(LEVELS)):
        gradient = level_backward(conv_weights[level_index], coupling[level_index, 0], pre_acts[level_index],
                                  start_cot[level_index], incoming, dilation)
        results[level_index] = gradient.astype(jnp.bfloat16)
        incoming = jnp.sum(coupling[level_index, 1].astype(jnp.float32)[None, :, None] * gradient, axis=1)
    return jnp.stack(results)
```

```python
import functools

import jax
import jax.numpy as jnp
from jax import lax
from jax.experimental import pallas as pl
from jax.experimental.pallas import tpu as pltpu
from jax.sharding import PartitionSpec as P

MESH = pl.DeviceIdType.MESH
BF = jnp.bfloat16
F32 = jnp.float32
DMAX = 16
AROUND = [(dr, dc) for dr in (-1, 0, 1) for dc in (-1, 0, 1) if (dr, dc) != (0, 0)]
NINE = [(0, 0)] + AROUND
NT = (((1,), (1,)), ((), ()))


def kernel(
    shape,
    dil,
    pre,
    cot,
    occ,
    w,
    coup,
    out,
    pre_e,
    pre0,
    pack,
    rim,
    s_own,
    s_in,
    shifted,
    m0_e,
    pack0,
    rim0,
    shifted0,
    grad1,
    totals,
    pmap,
    cmap,
    q_tile,
    q_side,
    in_tile,
    in_side,
    in_row,
    in_corner,
    w1l,
    w0l,
    vb,
    cb,
    out_v,
    local_sem,
    a_send,
    a_recv,
    s_send,
    s_recv,
    q_send,
    q_recv,
    m_send,
    m_recv,
):
    n_row, n_col, n_level = shape
    rows, chans, cols = 64, 64, 128
    ext = rows + 2 * DMAX
    row = lax.axis_index("row")
    col = lax.axis_index("col")
    level = lax.axis_index("level")

    def exists(dr, dc):
        return (
            (row + dr >= 0) & (row + dr < n_row) & (col + dc >= 0) & (col + dc < n_col)
        )

    def peer(dr, dc, dl=0):
        return {"row": row + dr, "col": col + dc, "level": level + dl}

    def remote(src, dst, send, recv, device):
        return pltpu.make_async_remote_copy(
            src_ref=src,
            dst_ref=dst,
            send_sem=send,
            recv_sem=recv,
            device_id=device,
            device_id_type=MESH,
        )

    load1 = pltpu.make_async_copy(pre.at[1], pre_e.at[pl.ds(DMAX, rows)], local_sem.at[0])
    load0 = pltpu.make_async_copy(pre.at[0], pre0, local_sem.at[1])
    load1.start()
    load0.start()

    for ref in (s_in, in_tile, in_side, in_row, in_corner):
        ref[...] = jnp.zeros_like(ref)

    barrier = pltpu.get_barrier_semaphore()
    for dr, dc in AROUND:

        @pl.when(exists(dr, dc))
        def _():
            pl.semaphore_signal(barrier, inc=1, device_id=peer(dr, dc), device_id_type=MESH)

    for dr, dc in NINE:

        @pl.when(exists(dr, dc) & (level + 1 < n_level))
        def _():
            pl.semaphore_signal(
                barrier, inc=1, device_id=peer(dr, dc, 1), device_id_type=MESH
            )

    count_r = jnp.where(row > 0, 1, 0) + 1 + jnp.where(row + 1 < n_row, 1, 0)
    count_c = jnp.where(col > 0, 1, 0) + 1 + jnp.where(col + 1 < n_col, 1, 0)
    around = count_r * count_c
    expected = around - 1 + jnp.where(level > 0, around, 0)

    for side, cond in ((0, row == 0), (1, row + 1 == n_row)):

        @pl.when(cond)
        def _():
            span = pl.ds(0 if side == 0 else DMAX + rows, DMAX)
            pre_e[span] = jnp.zeros((DMAX, chans, cols), BF)
            m0_e[span] = jnp.zeros((DMAX, chans, cols), BF)
            groups = pl.ds(0 if side == 0 else 10, 2)
            for lr in (0, 1):
                rim[lr, groups] = jnp.zeros((2, chans, cols), BF)
                rim0[lr, groups] = jnp.zeros((2, chans, cols), BF)

    for side, cond in ((0, col == 0), (1, col + 1 == n_col)):

        @pl.when(cond)
        def _():
            rim[side] = jnp.zeros((12, chans, cols), BF)
            rim0[side] = jnp.zeros((12, chans, cols), BF)

    own = jnp.where(occ[...] > 0, cot[...].astype(F32), 0.0).astype(BF)
    s_own[...] = own
    s_in[1, pl.ds(DMAX, rows)] = own

    pl.semaphore_wait(barrier, expected)

    src_rows = {1: (48, 16), 0: (0, 64), -1: (0, 16)}
    dst_rows = {1: (0, 16), 0: (16, 64), -1: (80, 16)}
    src_grps = {1: (6, 2), 0: (0, 8), -1: (0, 2)}
    dst_grps = {1: (0, 2), 0: (2, 8), -1: (10, 2)}

    def small_copies():
        found = []
        for k, (dr, dc) in enumerate(AROUND):
            found.append(
                (
                    (dr, dc),
                    remote(
                        s_own.at[pl.ds(*src_rows[dr])],
                        s_in.at[1 - dc, pl.ds(*dst_rows[dr])],
                        s_send.at[k],
                        s_recv.at[k],
                        peer(dr, dc),
                    ),
                )
            )
        return found

    def rim_copies(source, full, packed, rims, send, recv, offset):
        found = []
        for k, (dr, dc) in enumerate(AROUND):
            if dc == 0:
                start, size = src_rows[dr]
                src = source.at[pl.ds(start + offset, size)]
                dst = full.at[pl.ds(*dst_rows[dr])]
            else:
                src = packed.at[1 if dc == 1 else 0, pl.ds(*src_grps[dr])]
                dst = rims.at[0 if dc == 1 else 1, pl.ds(*dst_grps[dr])]
            found.append(((dr, dc), remote(src, dst, send.at[k], recv.at[k], peer(dr, dc))))
        return found

    def start(copies, which):
        for (dr, dc), copy in copies:
            if which(dr, dc):

                @pl.when(exists(dr, dc))
                def _():
                    copy.start()

    def wait_recv(copies, which=lambda dr, dc: True):
        for (dr, dc), copy in copies:
            if which(dr, dc):

                @pl.when(exists(-dr, -dc))
                def _():
                    copy.wait_recv()

    def wait_send(copies):
        for (dr, dc), copy in copies:

            @pl.when(exists(dr, dc))
            def _():
                copy.wait_send()

    a_copies = rim_copies(pre.at[1], pre_e, pack, rim, a_send, a_recv, 0)
    s_copies = small_copies()
    start(a_copies, lambda dr, dc: dc == 0)
    start(s_copies, lambda dr, dc: True)

    lane = lax.broadcasted_iota(jnp.int32, (chans, cols), 1)
    lane_e = lax.broadcasted_iota(jnp.int32, (ext, cols), 1)

    def pack_group(source, base, target, g):
        left = jnp.zeros((chans, cols), BF)
        right = jnp.zeros((chans, cols), BF)
        for i in range(8):
            value = source[base + g * 8 + i]
            if i:
                value = pltpu.roll(value, 16 * i, 1)
            left = jnp.where(lane // 16 == i, value, left)
            right = jnp.where(lane // 16 == (i + 7) % 8, value, right)
        target[0, g] = left
        target[1, g] = right

    def unpacked(rims, g, i):
        value = jnp.where(lane // 16 == i, rims[1, g], rims[0, g])
        if i:
            value = pltpu.roll(value, cols - 16 * i, 1)
        return value

    def side_shift(tile, halo, index, d):
        if index == 0:
            return pltpu.roll(jnp.where(index_lane(tile) >= d, tile, halo), cols - d, 1)
        return pltpu.roll(jnp.where(index_lane(tile) < cols - d, tile, halo), d, 1)

    def index_lane(value):
        return lane if value.shape[0] == chans else lane_e

    d1 = dil[1]
    d0 = dil[0]

    load1.wait()

    @pl.loop(0, 8)
    def _(g):
        pack_group(pre_e, DMAX, pack, g)

    start(a_copies, lambda dr, dc: dc != 0)

    eye = jnp.where(
        lax.broadcasted_iota(jnp.int32, (chans, chans), 0)
        == lax.broadcasted_iota(jnp.int32, (chans, chans), 1),
        1.0,
        0.0,
    ).astype(F32)
    eye_b = eye.astype(BF)
    w1l[...] = lax.dot_general(eye_b, w[1], NT, preferred_element_type=F32).astype(BF)
    w0l[...] = lax.dot_general(eye_b, w[0], NT, preferred_element_type=F32).astype(BF)
    c0row = coup[0:1, :].astype(F32)
    c1row = coup[1:2, :].astype(F32)
    c0col = jnp.dot(
        (eye * c0row).astype(BF), jnp.ones((chans, cols), BF), preferred_element_type=F32
    )
    c0col_b = c0col.astype(BF)
    c1rows = jnp.broadcast_to(c1row, (8, chans)).astype(BF)
    diag = (
        lax.broadcasted_iota(jnp.int32, (8, 8 * chans), 1) // chans
        == lax.broadcasted_iota(jnp.int32, (8, 8 * chans), 0)
    )
    for t in range(9):
        wt = w[0, pl.ds(t * chans, chans), :]
        wide = lax.dot_general(
            c1rows, jnp.concatenate([wt] * 8, axis=0), NT, preferred_element_type=F32
        )
        vb[pl.ds(8 * t, 8), :] = jnp.where(diag, wide, 0.0)
    wide = lax.dot_general(
        c1rows, jnp.concatenate([eye_b] * 8, axis=0), NT, preferred_element_type=F32
    )
    cb[...] = jnp.where(diag, wide, 0.0)
    for t in range(9):
        pmap[t] = jnp.zeros((rows + 4 * DMAX, cols), F32)
    cmap[...] = jnp.zeros_like(cmap)

    wait_recv(a_copies)

    @pl.loop(0, 12)
    def _(g):
        for i in range(8):
            tile = pre_e[g * 8 + i]
            halo = unpacked(rim, g, i)
            tile = jnp.where(tile > 0, c0col_b, 0)
            halo = jnp.where(halo > 0, c0col_b, 0)
            e = g * 8 + i
            shifted[e, pl.ds(0, chans), :] = side_shift(tile, halo, 0, d1)
            shifted[e, pl.ds(chans, chans), :] = tile
            shifted[e, pl.ds(2 * chans, chans), :] = side_shift(tile, halo, 2, d1)

    load0.wait()
    wait_recv(s_copies)

    q_copies = []
    for k, (dr, dc) in enumerate(NINE):
        e_src = {1: (64, 32), 0: (0, 96), -1: (0, 32)}[dr]
        if dc == 0:
            src = q_tile.at[:, pl.ds(*e_src)]
            dst = in_tile if dr == 0 else in_row.at[(1 - dr) // 2]
        else:
            src = q_side.at[(1 - dc) // 2, pl.ds(*e_src)]
            dst = in_side.at[(1 - dc) // 2] if dr == 0 else in_corner.at[(1 - dc) // 2, (1 - dr) // 2]
        q_copies.append(((dr, dc), remote(src, dst, q_send.at[k], q_recv.at[k], peer(dr, dc, -1))))

    for (dr, dc), copy in q_copies:

        @pl.when(exists(-dr, -dc) & (level + 1 < n_level))
        def _():
            copy.wait_recv()

    low = lane_e < DMAX
    high = lane_e >= cols - DMAX
    gap = jnp.zeros((rows - 2 * DMAX, cols), F32)

    def around_rows(above, below):
        return jnp.concatenate([above.astype(F32), gap, below.astype(F32)], axis=0)

    left = in_side[0].astype(F32) + around_rows(in_corner[0, 0], in_corner[0, 1])
    right = in_side[1].astype(F32) + around_rows(in_corner[1, 0], in_corner[1, 1])
    tile = in_tile[0].astype(F32) + around_rows(in_row[0, 0], in_row[1, 0])
    tile += jnp.where(low, left, 0.0) + jnp.where(high, right, 0.0)
    tile += s_in[1].astype(F32)
    halo = in_tile[1].astype(F32) + around_rows(in_row[0, 1], in_row[1, 1])
    halo += jnp.where(low, right, 0.0) + jnp.where(high, left, 0.0)
    halo += jnp.where(low, s_in[2].astype(F32), s_in[0].astype(F32))
    totals[0] = side_shift(tile, halo, 0, d1)
    totals[1] = tile
    totals[2] = side_shift(tile, halo, 2, d1)

    @pl.loop(0, rows // 4)
    def _(step):
        wide_in = []
        for i in range(4):
            r = step * 4 + i
            parts = []
            for a in (-1, 0, 1):
                e = r + DMAX - a * d1
                for b in range(3):
                    line = jnp.broadcast_to(totals[b, pl.ds(e, 1), :], (chans, cols)).astype(BF)
                    parts.append(shifted[e, pl.ds(b * chans, chans), :] * line)
            wide_in.append(jnp.concatenate(parts, axis=0))
        result = jnp.dot(
            w1l[...], jnp.concatenate(wide_in, axis=1), preferred_element_type=F32
        )
        for i in range(4):
            r = step * 4 + i
            value = result[:, i * cols : (i + 1) * cols]
            value += c0col * totals[1, pl.ds(r + DMAX, 1), :]
            grad1[r] = value
            m0_e[r + DMAX] = jnp.where(pre0[r] > 0, value.astype(BF), 0)

    m_copies = rim_copies(m0_e, m0_e, pack0, rim0, m_send, m_recv, DMAX)
    @pl.when(level > 0)
    def _():
        @pl.loop(0, 8)
        def _(g):
            first = jnp.concatenate([m0_e[DMAX + g * 8 + i] for i in range(8)], axis=0)
            maps = jnp.dot(vb[...].astype(BF), first, preferred_element_type=F32)
            second = jnp.concatenate([grad1[g * 8 + i].astype(BF) for i in range(8)], axis=0)
            center = jnp.dot(cb[...].astype(BF), second, preferred_element_type=F32)
            at = pl.ds(pl.multiple_of(g * 8, 8) + 2 * DMAX, 8)
            for t in range(9):
                pmap[t, at, :] = maps[8 * t : 8 * t + 8]
            cmap[pl.ds(pl.multiple_of(g * 8, 8) + DMAX, 8), :] = center

        def column(b):
            found = None
            for a in (-1, 0, 1):
                piece = pmap[(a + 1) * 3 + b + 1, pl.ds(DMAX - a * d0, ext), :]
                found = piece if found is None else found + piece
            return found

        goes_left = pltpu.roll(column(-1), cols - d0, 1)
        goes_right = pltpu.roll(column(1), d0, 1)
        q0 = cmap[...] + column(0)
        q0 += jnp.where(lane_e < cols - d0, goes_left, 0.0)
        q0 += jnp.where(lane_e >= d0, goes_right, 0.0)
        q1 = jnp.where(lane_e >= cols - d0, goes_left, 0.0)
        q1 += jnp.where(lane_e < d0, goes_right, 0.0)
        q_tile[0] = q0.astype(BF)
        q_tile[1] = q1.astype(BF)
        q_side[0] = jnp.where(low, q1, jnp.where(high, q0, 0.0)).astype(BF)
        q_side[1] = jnp.where(high, q1, jnp.where(low, q0, 0.0)).astype(BF)
        for (dr, dc), copy in q_copies:

            @pl.when(exists(dr, dc))
            def _():
                copy.start()

    start(m_copies, lambda dr, dc: dc == 0)

    @pl.loop(0, 8)
    def _(g):
        pack_group(m0_e, DMAX, pack0, g)

    start(m_copies, lambda dr, dc: dc != 0)
    wait_recv(m_copies)

    @pl.loop(0, 12)
    def _(g):
        for i in range(8):
            e = g * 8 + i
            tile = m0_e[e]
            halo = unpacked(rim0, g, i)
            shifted0[e, pl.ds(0, chans), :] = side_shift(tile, halo, 0, d0)
            shifted0[e, pl.ds(chans, chans), :] = tile
            shifted0[e, pl.ds(2 * chans, chans), :] = side_shift(tile, halo, 2, d0)

    @pl.loop(0, rows // 4)
    def _(step):
        wide_in = []
        for i in range(4):
            r = step * 4 + i
            parts = [shifted0[r + DMAX - a * d0] for a in (-1, 0, 1)]
            wide_in.append(jnp.concatenate(parts, axis=0))
        result = jnp.dot(
            w0l[...], jnp.concatenate(wide_in, axis=1), preferred_element_type=F32
        )
        for i in range(4):
            r = step * 4 + i
            out_v[r] = (grad1[r] + result[:, i * cols : (i + 1) * cols]).astype(BF)

    store = pltpu.make_async_copy(out_v, out, local_sem.at[2])
    store.start()
    wait_send(a_copies)
    wait_send(s_copies)
    wait_send(m_copies)

    @pl.when(level > 0)
    def _():
        wait_send(q_copies)

    store.wait()


def solution(mesh):
    shape = (mesh.shape["row"], mesh.shape["col"], mesh.shape["level"])

    def on_device(pre_acts, pred_cot, occupancy, conv_weights, coupling, dilation):
        vmem = pl.BlockSpec(memory_space=pltpu.VMEM)
        hbm = pl.BlockSpec(memory_space=pl.ANY)
        smem = pl.BlockSpec(memory_space=pltpu.SMEM)
        dma = pltpu.SemaphoreType.DMA
        result = pl.pallas_call(
            functools.partial(kernel, shape),
            out_shape=jax.ShapeDtypeStruct((64, 64, 128), BF),
            in_specs=[smem, hbm, vmem, vmem, vmem, vmem],
            out_specs=hbm,
            scratch_shapes=[
                pltpu.VMEM((96, 64, 128), BF),
                pltpu.VMEM((64, 64, 128), BF),
                pltpu.VMEM((2, 8, 64, 128), BF),
                pltpu.VMEM((2, 12, 64, 128), BF),
                pltpu.VMEM((64, 128), BF),
                pltpu.VMEM((3, 96, 128), BF),
                pltpu.VMEM((96, 192, 128), BF),
                pltpu.VMEM((96, 64, 128), BF),
                pltpu.VMEM((2, 8, 64, 128), BF),
                pltpu.VMEM((2, 12, 64, 128), BF),
                pltpu.VMEM((96, 192, 128), BF),
                pltpu.VMEM((64, 64, 128), F32),
                pltpu.VMEM((3, 96, 128), F32),
                pltpu.VMEM((9, 128, 128), F32),
                pltpu.VMEM((96, 128), F32),
                pltpu.VMEM((2, 96, 128), BF),
                pltpu.VMEM((2, 96, 128), BF),
                pltpu.VMEM((2, 96, 128), BF),
                pltpu.VMEM((2, 96, 128), BF),
                pltpu.VMEM((2, 2, 32, 128), BF),
                pltpu.VMEM((2, 2, 32, 128), BF),
                pltpu.VMEM((64, 576), BF),
                pltpu.VMEM((64, 576), BF),
                pltpu.VMEM((72, 512), F32),
                pltpu.VMEM((8, 512), F32),
                pltpu.VMEM((64, 64, 128), BF),
                dma((3,)),
                dma((8,)),
                dma((8,)),
                dma((8,)),
                dma((8,)),
                dma((9,)),
                dma((9,)),
                dma((8,)),
                dma((8,)),
            ],
            compiler_params=pltpu.CompilerParams(
                collective_id=0, has_side_effects=True, vmem_limit_bytes=48 * 2**20
            ),
        )(
            dilation,
            pre_acts.reshape(2, 64, 64, 128),
            pred_cot.reshape(64, 128),
            occupancy.reshape(64, 128),
            conv_weights.reshape(2, 576, 64),
            coupling.reshape(2, 64),
        )
        return result[None]

    return jax.shard_map(
        on_device,
        mesh=mesh,
        in_specs=(
            P("level", None, "row", None, "col"),
            P("level", "row", "col"),
            P("level", "row", "col"),
            P("level", None, None, None, None, None),
            P("level", None, None),
            P(),
        ),
        out_specs=P("level", "row", None, "col"),
        check_vma=False,
    )
```

```python
import functools

import jax
import jax.numpy as jnp
from jax import lax
from jax.experimental import pallas as pl
from jax.experimental.pallas import tpu as pltpu
from jax.sharding import PartitionSpec as P

MESH = pl.DeviceIdType.MESH
BF = jnp.bfloat16
F32 = jnp.float32
DMAX = 16
AROUND = [(dr, dc) for dr in (-1, 0, 1) for dc in (-1, 0, 1) if (dr, dc) != (0, 0)]
NINE = [(0, 0)] + AROUND
NT = (((1,), (1,)), ((), ()))


def kernel(
    shape,
    dil,
    pre,
    cot_hbm,
    occ_hbm,
    w_hbm,
    coup_hbm,
    out,
    cot,
    occ,
    w,
    coup,
    pre_e,
    pre0,
    pack,
    rim,
    s_own,
    s_in,
    shifted,
    m0,
    m0_e,
    pack0,
    rim0,
    grad1,
    totals,
    pmap,
    cmap,
    q_msg,
    q_side,
    in_tile,
    in_side,
    in_row,
    in_corner,
    w1l,
    w1t,
    tmap,
    tcen,
    w0o,
    vb,
    cb,
    out_v,
    local_sem,
    out_sem,
    a_send,
    a_recv,
    s_send,
    s_recv,
    q_send,
    q_recv,
    m_send,
    m_recv,
):
    n_row, n_col, n_level = shape
    rows, chans, cols = 64, 64, 128
    ext = rows + 2 * DMAX
    row = lax.axis_index("row")
    col = lax.axis_index("col")
    level = lax.axis_index("level")

    def exists(dr, dc):
        return (
            (row + dr >= 0) & (row + dr < n_row) & (col + dc >= 0) & (col + dc < n_col)
        )

    def peer(dr, dc, dl=0):
        return {"row": row + dr, "col": col + dc, "level": level + dl}

    def remote(src, dst, send, recv, device):
        return pltpu.make_async_remote_copy(
            src_ref=src,
            dst_ref=dst,
            send_sem=send,
            recv_sem=recv,
            device_id=device,
            device_id_type=MESH,
        )

    loads = [
        pltpu.make_async_copy(src, dst, local_sem.at[i])
        for i, (src, dst) in enumerate(
            (
                (pre.at[1], pre_e.at[pl.ds(DMAX, rows)]),
                (cot_hbm, cot),
                (occ_hbm, occ),
                (w_hbm, w),
                (coup_hbm, coup),
                (pre.at[0], pre0),
            )
        )
    ]
    for load in loads:
        load.start()

    for ref in (s_in, in_tile, in_side, in_row, in_corner):
        ref[...] = jnp.zeros_like(ref)

    barrier = pltpu.get_barrier_semaphore()
    for dr, dc in AROUND:

        @pl.when(exists(dr, dc))
        def _():
            pl.semaphore_signal(barrier, inc=1, device_id=peer(dr, dc), device_id_type=MESH)

    for dr, dc in NINE:

        @pl.when(exists(dr, dc) & (level + 1 < n_level))
        def _():
            pl.semaphore_signal(
                barrier, inc=1, device_id=peer(dr, dc, 1), device_id_type=MESH
            )

    count_r = jnp.where(row > 0, 1, 0) + 1 + jnp.where(row + 1 < n_row, 1, 0)
    count_c = jnp.where(col > 0, 1, 0) + 1 + jnp.where(col + 1 < n_col, 1, 0)
    around = count_r * count_c
    expected = around - 1 + jnp.where(level > 0, around, 0)

    for side, cond in ((0, row == 0), (1, row + 1 == n_row)):

        @pl.when(cond)
        def _():
            span = pl.ds(0 if side == 0 else DMAX + rows, DMAX)
            pre_e[span] = jnp.zeros((DMAX, chans, cols), BF)
            m0_e[span] = jnp.zeros((DMAX, chans, cols), BF)
            groups = pl.ds(0 if side == 0 else 10, 2)
            for lr in (0, 1):
                rim[lr, groups] = jnp.zeros((2, chans, cols), BF)

    for side, cond in ((0, col == 0), (1, col + 1 == n_col)):

        @pl.when(cond)
        def _():
            rim[side] = jnp.zeros((12, chans, cols), BF)
            rim0[1 - side] = jnp.zeros((8, chans, cols), BF)

    src_rows = {1: (48, 16), 0: (0, 64), -1: (0, 16)}
    dst_rows = {1: (0, 16), 0: (16, 64), -1: (80, 16)}

    def row_copy(source, full, send, recv, offset, dr):
        start, size = src_rows[dr]
        k = (1 - dr) // 2
        return remote(
            source.at[pl.ds(start + offset, size)],
            full.at[pl.ds(*dst_rows[dr])],
            send.at[k],
            recv.at[k],
            peer(dr, 0),
        )

    def corner_copy(packed, rims, send, recv, dr, dc):
        k = 2 + (1 - dr) + (1 - dc) // 2
        return remote(
            packed.at[(1 + dc) // 2, pl.ds(6 if dr == 1 else 0, 2)],
            rims.at[(1 - dc) // 2, pl.ds(0 if dr == 1 else 10, 2)],
            send.at[k],
            recv.at[k],
            peer(dr, dc),
        )

    def side_copy(packed, rims, send, recv, dc):
        return remote(
            packed.at[(1 + dc) // 2],
            rims.at[(1 - dc) // 2, pl.ds(2, 8)],
            send.at[6 + (1 - dc) // 2],
            recv.at[6 + (1 - dc) // 2],
            peer(0, dc),
        )

    def when_started(dr, dc, act):
        @pl.when(exists(dr, dc))
        def _():
            act()

    def when_expected(dr, dc, act):
        @pl.when(exists(-dr, -dc))
        def _():
            act()

    early_rows = {dr: row_copy(pre.at[1], pre_e, a_send, a_recv, 0, dr) for dr in (1, -1)}
    early_sides = {dc: side_copy(pack, rim, a_send, a_recv, dc) for dc in (1, -1)}
    early_corners = {
        (dr, dc): corner_copy(pack, rim, a_send, a_recv, dr, dc) for dr in (1, -1) for dc in (1, -1)
    }
    late_rows = {dr: row_copy(m0, m0_e, m_send, m_recv, 0, dr) for dr in (1, -1)}

    def late_side(chunk, dc):
        k = 2 + 4 * ((1 - dc) // 2) + chunk
        return remote(
            pack0.at[(1 + dc) // 2, pl.ds(2 * chunk, 2)],
            rim0.at[(1 + dc) // 2, pl.ds(2 * chunk, 2)],
            m_send.at[k],
            m_recv.at[k],
            peer(0, dc),
        )

    def start_late_rows():
        for dr, copy in late_rows.items():
            when_started(dr, 0, copy.start)

    lane = lax.broadcasted_iota(jnp.int32, (DMAX, cols), 1).astype(F32).astype(BF)
    lane = jnp.concatenate([lane] * (chans // DMAX), axis=0)
    lane_e = lax.broadcasted_iota(jnp.int32, (ext, cols), 1)
    lane_b = lax.broadcasted_iota(jnp.int32, (32, cols), 1)

    def pack_rows(values):
        turns = [values[0]]
        for i in range(1, 8):
            turns.append(pltpu.roll(values[i], 16 * i, 1))
        left, right = turns[7], turns[0]
        for i in range(6, -1, -1):
            inside = lane < 16 * (i + 1)
            left = jnp.where(inside, turns[i], left)
            right = jnp.where(inside, turns[i + 1], right)
        return left, right

    def unpacked(rims, g, i):
        value = jnp.where((lane >= 16 * i) & (lane < 16 * i + 16), rims[1, g], rims[0, g])
        if i:
            value = pltpu.roll(value, cols - 16 * i, 1)
        return value

    d1 = dil[1]
    d0 = dil[0]

    def splat(value):
        return jnp.full((chans, cols), value.astype(F32)).astype(BF)

    def side_shift(tile, halo, index, d):
        if tile.shape[0] == chans:
            where, split = lane, splat(d if index == 0 else cols - d)
        else:
            where, split = lane_e, d if index == 0 else cols - d
        if index == 0:
            return pltpu.roll(jnp.where(where >= split, tile, halo), cols - d, 1)
        return pltpu.roll(jnp.where(where < split, tile, halo), d, 1)

    loads[0].wait()

    @pl.loop(0, 4)
    def _(chunk):
        for half in (0, 1):
            g = 2 * chunk + half
            left, right = pack_rows([pre_e[DMAX + 8 * g + i] for i in range(8)])
            pack[0, g] = left
            pack[1, g] = right

    pl.semaphore_wait(barrier, expected)
    for dc, copy in early_sides.items():
        when_started(0, dc, copy.start)
    for dr, copy in early_rows.items():
        when_started(dr, 0, copy.start)
    for (dr, dc), copy in early_corners.items():
        when_started(dr, dc, copy.start)

    loads[1].wait()
    loads[2].wait()
    own = jnp.where(occ[...] > 0, cot[...].astype(F32), 0.0).astype(BF)
    s_own[...] = own
    s_in[1, pl.ds(DMAX, rows)] = own
    s_copies = []
    for k, (dr, dc) in enumerate(AROUND):
        copy = remote(
            s_own.at[pl.ds(*src_rows[dr])],
            s_in.at[1 - dc, pl.ds(*dst_rows[dr])],
            s_send.at[k],
            s_recv.at[k],
            peer(dr, dc),
        )
        s_copies.append(((dr, dc), copy))
        when_started(dr, dc, copy.start)

    loads[3].wait()
    loads[4].wait()
    eye = jnp.where(
        lax.broadcasted_iota(jnp.int32, (chans, chans), 0)
        == lax.broadcasted_iota(jnp.int32, (chans, chans), 1),
        1.0,
        0.0,
    ).astype(F32)
    eye_b = eye.astype(BF)

    def tap(t):
        return w[0, pl.ds(t * chans, chans), :]

    def turned(value):
        return lax.dot_general(eye_b, value, NT, preferred_element_type=F32).astype(BF)

    w1l[...] = turned(w[1])
    c0row = coup[0:1, :].astype(F32)
    c1row = coup[1:2, :].astype(F32)
    c0col = jnp.dot(
        (eye * c0row).astype(BF), jnp.ones((chans, cols), BF), preferred_element_type=F32
    )
    c0col_b = c0col.astype(BF)
    c1rows = jnp.broadcast_to(c1row, (8, chans))
    diag = (
        lax.broadcasted_iota(jnp.int32, (8, 8 * chans), 1) // chans
        == lax.broadcasted_iota(jnp.int32, (8, 8 * chans), 0)
    )
    heads = lax.dot_general(
        c1rows.astype(BF), w[0], NT, preferred_element_type=F32
    )
    for b in range(3):
        w0o[pl.ds(b * chans, chans), :] = turned(
            jnp.concatenate([tap(3 * a + b) for a in range(3)], axis=0)
        )

    def spread(value):
        return jnp.where(diag, jnp.concatenate([value] * 8, axis=1), 0.0)

    vb[...] = jnp.concatenate(
        [spread(heads[:, t * chans : (t + 1) * chans]) for t in range(9)], axis=0
    ).astype(BF)
    cb[...] = jnp.concatenate([spread(c1rows)] * 2, axis=0).astype(BF)
    for t in range(9):
        for start in (DMAX, 2 * DMAX + rows):
            pmap[t, pl.ds(start, DMAX), :] = jnp.zeros((DMAX, cols), F32)
            pmap[t, pl.ds(start - DMAX if start == DMAX else start + DMAX, DMAX), :] = (
                jnp.zeros((DMAX, cols), F32)
            )
    for start in (0, DMAX + rows):
        cmap[pl.ds(start, DMAX), :] = jnp.zeros((DMAX, cols), F32)

    for dr, copy in early_rows.items():
        when_expected(dr, 0, copy.wait_recv)
    for dc, copy in early_sides.items():
        when_expected(0, dc, copy.wait_recv)
    for (dr, dc), copy in early_corners.items():
        when_expected(dr, dc, copy.wait_recv)

    @pl.loop(0, 3)
    def _(part):
        for quarter in range(4):
            g = part * 4 + quarter
            for i in range(8):
                e = g * 8 + i
                tile = jnp.where(pre_e[e] > 0, c0col_b, 0)
                halo = jnp.where(unpacked(rim, g, i) > 0, c0col_b, 0)
                shifted[e, pl.ds(0, chans), :] = side_shift(tile, halo, 0, d1)
                shifted[e, pl.ds(chans, chans), :] = tile
                shifted[e, pl.ds(2 * chans, chans), :] = side_shift(tile, halo, 2, d1)

    loads[5].wait()

    middle = (level > 0) & (level + 1 < n_level)

    @pl.when(middle)
    def _():
        for t in range(9):
            w1t[t] = turned(w[1, pl.ds(t * chans, chans), :])

        @pl.loop(0, 4)
        def _(chunk):
            keep = [pre0[chunk * 16 + i] > 0 for i in range(16)]
            for t in range(10):
                if t < 9:
                    taps_in = jnp.concatenate(
                        [
                            shifted[
                                chunk * 16 + i + DMAX - (t // 3 - 1) * d1,
                                pl.ds((t % 3) * chans, chans),
                                :,
                            ]
                            for i in range(16)
                        ],
                        axis=1,
                    )
                    made = jnp.dot(w1t[t], taps_in, preferred_element_type=F32).astype(BF)
                    pieces = [made[:, i * cols : (i + 1) * cols] for i in range(16)]
                else:
                    pieces = [c0col_b] * 16
                kept = [jnp.where(keep[i], pieces[i], 0) for i in range(16)]
                for target, lhs, values in ((tmap, vb, kept), (tcen, cb, pieces)):
                    rhs = jnp.concatenate(
                        [
                            jnp.concatenate(values[0:8], axis=0),
                            jnp.concatenate(values[8:16], axis=0),
                        ],
                        axis=1,
                    )
                    maps = jnp.dot(lhs[...], rhs, preferred_element_type=F32)
                    size = target.shape[2]
                    target[t, 2 * chunk] = maps[0:size, 0:cols]
                    target[t, 2 * chunk + 1] = maps[0:size, cols : 2 * cols]

    for (dr, dc), copy in s_copies:
        when_expected(dr, dc, copy.wait_recv)

    q_copies = []
    for k, (dr, dc) in enumerate(NINE):
        if dc == 0:
            src = q_msg.at[pl.ds(*{1: (96, 64), 0: (32, 128), -1: (0, 64)}[dr])]
            dst = in_tile if dr == 0 else in_row.at[(1 - dr) // 2]
        else:
            src = q_side.at[(1 - dc) // 2]
            dst = in_side.at[(1 - dc) // 2] if dr == 0 else in_corner.at[(1 - dc) // 2, (1 - dr) // 2]
        q_copies.append(((dr, dc), remote(src, dst, q_send.at[k], q_recv.at[k], peer(dr, dc, -1))))

    for (dr, dc), copy in q_copies:

        @pl.when(exists(-dr, -dc) & (level + 1 < n_level))
        def _():
            copy.wait_recv()

    low = lane_e < DMAX
    high = lane_e >= cols - DMAX

    def folded(value):
        found = None
        for j in range(3):
            piece = pltpu.roll(value[32 * j : 32 * j + 32], DMAX + 32 * j, 1)
            found = piece if found is None else jnp.where(lane_b // 32 == j, piece, found)
        return found

    def unfolded(value, j):
        return pltpu.roll(value.astype(F32), cols - DMAX - 32 * j, 1)

    def summed(middle, above, below):
        return jnp.concatenate(
            [
                unfolded(middle, 0) + unfolded(above, 2),
                unfolded(middle, 1),
                unfolded(middle, 2) + unfolded(below, 0),
            ],
            axis=0,
        )

    left = summed(in_side[0], in_corner[0, 0], in_corner[0, 1])
    right = summed(in_side[1], in_corner[1, 0], in_corner[1, 1])
    edges = jnp.concatenate(
        [
            in_row[0, pl.ds(0, 32)].astype(F32),
            jnp.zeros((rows - 2 * DMAX, cols), F32),
            in_row[1, pl.ds(32, 32)].astype(F32),
        ],
        axis=0,
    )
    tile = in_tile[pl.ds(0, ext)].astype(F32) + edges + s_in[1].astype(F32)
    tile += jnp.where(low, left, 0.0) + jnp.where(high, right, 0.0)
    halo = summed(in_tile[pl.ds(ext, 32)], in_row[0, pl.ds(32, 32)], in_row[1, pl.ds(0, 32)])
    halo += jnp.where(low, right + s_in[2].astype(F32), left + s_in[0].astype(F32))
    totals[0] = side_shift(tile, halo, 0, d1)
    totals[1] = tile
    totals[2] = side_shift(tile, halo, 2, d1)

    def layer_1(chunk):
        for pair in range(8):
            wide_in = []
            for i in range(2):
                r = chunk * 16 + pair * 2 + i
                parts = []
                for a in (-1, 0, 1):
                    e = r + DMAX - a * d1
                    for b in range(3):
                        line = jnp.broadcast_to(totals[b, pl.ds(e, 1), :], (16, cols)).astype(BF)
                        line = jnp.concatenate([line] * 4, axis=0)
                        parts.append(shifted[e, pl.ds(b * chans, chans), :] * line)
                wide_in.append(jnp.concatenate(parts, axis=0))
            result = jnp.dot(
                w1l[...], jnp.concatenate(wide_in, axis=1), preferred_element_type=F32
            )
            for i in range(2):
                r = chunk * 16 + pair * 2 + i
                value = result[:, i * cols : (i + 1) * cols]
                value += c0col * totals[1, pl.ds(r + DMAX, 1), :]
                grad1[r] = value
                kept = jnp.where(pre0[r] > 0, value.astype(BF), 0)
                m0[r] = kept
                m0_e[r + DMAX] = kept

    def prediction_maps(chunk):
        for half in range(2):
            g = chunk * 2 + half
            first = jnp.concatenate([m0[g * 8 + i] for i in range(8)], axis=0)
            maps = jnp.dot(vb[...], first, preferred_element_type=F32)
            second = jnp.concatenate([grad1[g * 8 + i].astype(BF) for i in range(8)], axis=0)
            center = jnp.dot(cb[...], second, preferred_element_type=F32)
            at = pl.ds(pl.multiple_of(g * 8, 8) + 2 * DMAX, 8)
            for t in range(9):
                pmap[t, at, :] = maps[8 * t : 8 * t + 8]
            cmap[pl.ds(pl.multiple_of(g * 8, 8) + DMAX, 8), :] = center[0:8]

    def column(b):
        found = None
        for a in (-1, 0, 1):
            piece = pmap[(a + 1) * 3 + b + 1, pl.ds(DMAX - a * d0, ext), :]
            found = piece if found is None else found + piece
        return found

    @pl.when(level + 1 == n_level)
    def _():
        @pl.loop(0, 4)
        def _(chunk):
            layer_1(chunk)
            prediction_maps(chunk)

    @pl.when(middle)
    def _():
        @pl.loop(0, 4)
        def _(chunk):
            for half in range(2):
                g = chunk * 2 + half
                lines = [
                    totals[t % 3, pl.ds(g * 8 + DMAX - (t // 3 - 1) * d1, 8), :]
                    for t in range(9)
                ]
                lines.append(totals[1, pl.ds(pl.multiple_of(g * 8, 8) + DMAX, 8), :])
                start = pl.multiple_of(g * 8, 8)
                for k in range(9):
                    found = lines[0] * tmap[0, g, pl.ds(8 * k, 8), :]
                    for t in range(1, 10):
                        found += lines[t] * tmap[t, g, pl.ds(8 * k, 8), :]
                    pmap[k, pl.ds(start + 2 * DMAX, 8), :] = found
                found = lines[0] * tcen[0, g]
                for t in range(1, 10):
                    found += lines[t] * tcen[t, g]
                cmap[pl.ds(start + DMAX, 8), :] = found

    @pl.when(level > 0)
    def _():
        goes_left = pltpu.roll(column(-1), cols - d0, 1)
        goes_right = pltpu.roll(column(1), d0, 1)
        q0 = cmap[...] + column(0)
        q0 += jnp.where(lane_e < cols - d0, goes_left, 0.0)
        q0 += jnp.where(lane_e >= d0, goes_right, 0.0)
        q1 = jnp.where(lane_e >= cols - d0, goes_left, 0.0)
        q1 += jnp.where(lane_e < d0, goes_right, 0.0)
        q_side[0] = folded(jnp.where(low, q1, q0)).astype(BF)
        q_side[1] = folded(jnp.where(low, q0, q1)).astype(BF)
        rim_part = folded(q1).astype(BF)
        q_msg[pl.ds(0, 32)] = rim_part
        q_msg[pl.ds(32, ext)] = q0.astype(BF)
        q_msg[pl.ds(32 + ext, 32)] = rim_part
        for (dr, dc), copy in q_copies:
            when_started(dr, dc, copy.start)

    @pl.when(level + 1 < n_level)
    def _():
        @pl.loop(0, 4)
        def _(step):
            layer_1(jnp.where(step == 0, 0, jnp.where(step == 1, 3, step - 1)))

            @pl.when(step == 1)
            def _():
                start_late_rows()

    @pl.when(level + 1 == n_level)
    def _():
        start_late_rows()

    edge = (lane < DMAX) | (lane >= cols - DMAX)
    own_right = lane >= splat(d0)
    own_left = lane < splat(cols - d0)

    def store(chunk):
        span = pl.ds(chunk * 16, 16)
        return pltpu.make_async_copy(out_v.at[span], out.at[span], out_sem.at[chunk])

    def layer_0(chunk, source, offset):
        outer = []
        for pair in range(8):
            wide_in = []
            for i in range(2):
                r = chunk * 16 + pair * 2 + i
                wide_in.append(
                    jnp.concatenate([source[r + offset - a * d0] for a in (-1, 0, 1)], axis=0)
                )
            result = jnp.dot(
                w0o[...], jnp.concatenate(wide_in, axis=1), preferred_element_type=F32
            )
            for i in range(2):
                r = chunk * 16 + pair * 2 + i
                lanes = slice(i * cols, (i + 1) * cols)
                goes_left = pltpu.roll(result[0:chans, lanes].astype(BF), cols - d0, 1)
                goes_right = pltpu.roll(result[2 * chans :, lanes].astype(BF), d0, 1)
                outer.append(jnp.where(own_right, jnp.where(own_left, 0, goes_left), goes_right))
                value = grad1[r] + result[chans : 2 * chans, lanes]
                value += jnp.where(own_left, goes_left, 0).astype(F32)
                value += jnp.where(own_right, goes_right, 0).astype(F32)
                grad1[r] = value
        for half in range(2):
            to_right, to_left = pack_rows(outer[8 * half : 8 * half + 8])
            pack0[0, 2 * chunk + half] = to_left
            pack0[1, 2 * chunk + half] = to_right
        for dc in (1, -1):
            when_started(0, dc, late_side(chunk, dc).start)

    @pl.loop(0, 2)
    def _(step):
        layer_0(step + 1, m0, 0)

    for dr, copy in late_rows.items():
        when_expected(dr, 0, copy.wait_recv)

    @pl.loop(0, 2)
    def _(step):
        layer_0(step * 3, m0_e, DMAX)

    @pl.loop(0, 4)
    def _(step):
        chunk = jnp.where(step < 2, step + 1, jnp.where(step == 2, 0, 3))
        for dc in (1, -1):
            when_expected(0, dc, late_side(chunk, dc).wait_recv)
        for half in range(2):
            g = chunk * 2 + half
            for i in range(8):
                r = g * 8 + i
                extra = jnp.where(edge, unpacked(rim0, g, i), 0).astype(F32)
                out_v[r] = (grad1[r] + extra).astype(BF)
        store(chunk).start()

    for dr, copy in early_rows.items():
        when_started(dr, 0, copy.wait_send)
    for dc, copy in early_sides.items():
        when_started(0, dc, copy.wait_send)
    for (dr, dc), copy in early_corners.items():
        when_started(dr, dc, copy.wait_send)
    for dr, copy in late_rows.items():
        when_started(dr, 0, copy.wait_send)
    for dc in (1, -1):
        for chunk in range(4):
            when_started(0, dc, late_side(chunk, dc).wait_send)
    for (dr, dc), copy in s_copies:
        when_started(dr, dc, copy.wait_send)

    @pl.when(level > 0)
    def _():
        for (dr, dc), copy in q_copies:
            when_started(dr, dc, copy.wait_send)

    for chunk in range(4):
        store(chunk).wait()


def solution(mesh):
    shape = (mesh.shape["row"], mesh.shape["col"], mesh.shape["level"])

    def on_device(pre_acts, pred_cot, occupancy, conv_weights, coupling, dilation):
        hbm = pl.BlockSpec(memory_space=pl.ANY)
        smem = pl.BlockSpec(memory_space=pltpu.SMEM)
        dma = pltpu.SemaphoreType.DMA
        result = pl.pallas_call(
            functools.partial(kernel, shape),
            out_shape=jax.ShapeDtypeStruct((64, 64, 128), BF),
            in_specs=[smem, hbm, hbm, hbm, hbm, hbm],
            out_specs=hbm,
            scratch_shapes=[
                pltpu.VMEM((64, 128), BF),
                pltpu.VMEM((64, 128), jnp.int32),
                pltpu.VMEM((2, 576, 64), BF),
                pltpu.VMEM((2, 64), BF),
                pltpu.VMEM((96, 64, 128), BF),
                pltpu.VMEM((64, 64, 128), BF),
                pltpu.VMEM((2, 8, 64, 128), BF),
                pltpu.VMEM((2, 12, 64, 128), BF),
                pltpu.VMEM((64, 128), BF),
                pltpu.VMEM((3, 96, 128), BF),
                pltpu.VMEM((96, 192, 128), BF),
                pltpu.VMEM((64, 64, 128), BF),
                pltpu.VMEM((96, 64, 128), BF),
                pltpu.VMEM((2, 8, 64, 128), BF),
                pltpu.VMEM((2, 8, 64, 128), BF),
                pltpu.VMEM((64, 64, 128), F32),
                pltpu.VMEM((3, 96, 128), F32),
                pltpu.VMEM((9, 128, 128), F32),
                pltpu.VMEM((96, 128), F32),
                pltpu.VMEM((160, 128), BF),
                pltpu.VMEM((2, 32, 128), BF),
                pltpu.VMEM((128, 128), BF),
                pltpu.VMEM((2, 32, 128), BF),
                pltpu.VMEM((2, 64, 128), BF),
                pltpu.VMEM((2, 2, 32, 128), BF),
                pltpu.VMEM((64, 576), BF),
                pltpu.VMEM((9, 64, 64), BF),
                pltpu.VMEM((10, 8, 72, 128), F32),
                pltpu.VMEM((10, 8, 8, 128), F32),
                pltpu.VMEM((192, 192), BF),
                pltpu.VMEM((72, 512), BF),
                pltpu.VMEM((16, 512), BF),
                pltpu.VMEM((64, 64, 128), BF),
                dma((6,)),
                dma((4,)),
                dma((8,)),
                dma((8,)),
                dma((8,)),
                dma((8,)),
                dma((9,)),
                dma((9,)),
                dma((10,)),
                dma((10,)),
            ],
            compiler_params=pltpu.CompilerParams(
                collective_id=0, has_side_effects=True, vmem_limit_bytes=64 * 2**20
            ),
        )(
            dilation,
            pre_acts.reshape(2, 64, 64, 128),
            pred_cot.reshape(64, 128),
            occupancy.reshape(64, 128),
            conv_weights.reshape(2, 576, 64),
            coupling.reshape(2, 64),
        )
        return result[None]

    return jax.shard_map(
        on_device,
        mesh=mesh,
        in_specs=(
            P("level", None, "row", None, "col"),
            P("level", "row", "col"),
            P("level", "row", "col"),
            P("level", None, None, None, None, None),
            P("level", None, None),
            P(),
        ),
        out_specs=P("level", "row", None, "col"),
        check_vma=False,
    )
```

```python
import functools

import jax
import jax.numpy as jnp
from jax import lax
from jax.experimental import pallas as pl
from jax.experimental.pallas import tpu as pltpu
from jax.sharding import PartitionSpec as P

MESH = pl.DeviceIdType.MESH
BF = jnp.bfloat16
F32 = jnp.float32
DMAX = 16
AROUND = [(dr, dc) for dr in (-1, 0, 1) for dc in (-1, 0, 1) if (dr, dc) != (0, 0)]
NINE = [(0, 0)] + AROUND
NT = (((1,), (1,)), ((), ()))


def kernel(
    shape,
    dil,
    pre,
    cot_hbm,
    occ_hbm,
    w_hbm,
    coup_hbm,
    out,
    cot,
    occ,
    w,
    coup,
    pre_e,
    pre0,
    pack,
    rim,
    s_own,
    s_in,
    shifted,
    m0,
    m0_e,
    pack0,
    rim0,
    grad1,
    totals,
    pmap,
    cmap,
    q_msg,
    q_side,
    in_tile,
    in_side,
    in_row,
    in_corner,
    w1l,
    w1t,
    tmap,
    tcen,
    w0o,
    vb,
    cb,
    out_v,
    local_sem,
    out_sem,
    a_send,
    a_recv,
    s_send,
    s_recv,
    q_send,
    q_recv,
    m_send,
    m_recv,
):
    n_row, n_col, n_level = shape
    rows, chans, cols = 64, 64, 128
    ext = rows + 2 * DMAX
    row = lax.axis_index("row")
    col = lax.axis_index("col")
    level = lax.axis_index("level")

    def exists(dr, dc):
        return (
            (row + dr >= 0) & (row + dr < n_row) & (col + dc >= 0) & (col + dc < n_col)
        )

    def peer(dr, dc, dl=0):
        return {"row": row + dr, "col": col + dc, "level": level + dl}

    def remote(src, dst, send, recv, device):
        return pltpu.make_async_remote_copy(
            src_ref=src,
            dst_ref=dst,
            send_sem=send,
            recv_sem=recv,
            device_id=device,
            device_id_type=MESH,
        )

    loads = [
        pltpu.make_async_copy(src, dst, local_sem.at[i])
        for i, (src, dst) in enumerate(
            (
                (pre.at[1], pre_e.at[pl.ds(DMAX, rows)]),
                (cot_hbm, cot),
                (occ_hbm, occ),
                (w_hbm, w),
                (coup_hbm, coup),
                (pre.at[0], pre0),
            )
        )
    ]
    for load in loads:
        load.start()

    for ref in (s_in, in_tile, in_side, in_row, in_corner):
        ref[...] = jnp.zeros_like(ref)

    barrier = pltpu.get_barrier_semaphore()
    for dr, dc in AROUND:

        @pl.when(exists(dr, dc))
        def _():
            pl.semaphore_signal(barrier, inc=1, device_id=peer(dr, dc), device_id_type=MESH)

    for dr, dc in NINE:

        @pl.when(exists(dr, dc) & (level + 1 < n_level))
        def _():
            pl.semaphore_signal(
                barrier, inc=1, device_id=peer(dr, dc, 1), device_id_type=MESH
            )

    count_r = jnp.where(row > 0, 1, 0) + 1 + jnp.where(row + 1 < n_row, 1, 0)
    count_c = jnp.where(col > 0, 1, 0) + 1 + jnp.where(col + 1 < n_col, 1, 0)
    around = count_r * count_c
    expected = around - 1 + jnp.where(level > 0, around, 0)

    for side, cond in ((0, row == 0), (1, row + 1 == n_row)):

        @pl.when(cond)
        def _():
            span = pl.ds(0 if side == 0 else DMAX + rows, DMAX)
            pre_e[span] = jnp.zeros((DMAX, chans, cols), BF)
            m0_e[span] = jnp.zeros((DMAX, chans, cols), BF)
            groups = pl.ds(0 if side == 0 else 10, 2)
            for lr in (0, 1):
                rim[lr, groups] = jnp.zeros((2, chans, cols), BF)

    for side, cond in ((0, col == 0), (1, col + 1 == n_col)):

        @pl.when(cond)
        def _():
            rim[side] = jnp.zeros((12, chans, cols), BF)
            rim0[1 - side] = jnp.zeros((8, chans, cols), BF)

    src_rows = {1: (48, 16), 0: (0, 64), -1: (0, 16)}
    dst_rows = {1: (0, 16), 0: (16, 64), -1: (80, 16)}

    def row_copies(source, full, send, recv):
        found = []
        for dr in (1, -1):
            for part in range(4):
                k = 4 * ((1 - dr) // 2) + part
                copy = remote(
                    source.at[pl.ds(src_rows[dr][0] + 4 * part, 4)],
                    full.at[pl.ds(dst_rows[dr][0] + 4 * part, 4)],
                    send.at[k],
                    recv.at[k],
                    peer(dr, 0),
                )
                found.append((dr, copy))
        return found

    def corner_copy(packed, rims, send, recv, dr, dc):
        k = 8 + (1 - dr) + (1 - dc) // 2
        return remote(
            packed.at[(1 + dc) // 2, pl.ds(6 if dr == 1 else 0, 2)],
            rims.at[(1 - dc) // 2, pl.ds(0 if dr == 1 else 10, 2)],
            send.at[k],
            recv.at[k],
            peer(dr, dc),
        )

    def side_copy(packed, rims, send, recv, dc, chunk):
        k = 12 + 4 * ((1 - dc) // 2) + chunk
        return remote(
            packed.at[(1 + dc) // 2, pl.ds(2 * chunk, 2)],
            rims.at[(1 - dc) // 2, pl.ds(2 * chunk + 2, 2)],
            send.at[k],
            recv.at[k],
            peer(0, dc),
        )

    def when_started(dr, dc, act):
        @pl.when(exists(dr, dc))
        def _():
            act()

    def when_expected(dr, dc, act):
        @pl.when(exists(-dr, -dc))
        def _():
            act()

    early = [((dr, 0), copy) for dr, copy in row_copies(pre.at[1], pre_e, a_send, a_recv)]
    for chunk in range(4):
        for dc in (1, -1):
            early.append(((0, dc), side_copy(pack, rim, a_send, a_recv, dc, chunk)))
    for dr in (1, -1):
        for dc in (1, -1):
            early.append(((dr, dc), corner_copy(pack, rim, a_send, a_recv, dr, dc)))
    late_rows = row_copies(m0, m0_e, m_send, m_recv)

    def late_side(chunk, dc):
        k = 8 + 4 * ((1 - dc) // 2) + chunk
        return remote(
            pack0.at[(1 + dc) // 2, pl.ds(2 * chunk, 2)],
            rim0.at[(1 + dc) // 2, pl.ds(2 * chunk, 2)],
            m_send.at[k],
            m_recv.at[k],
            peer(0, dc),
        )

    def start_late_rows(which):
        for dr, copy in late_rows:
            if dr == which:
                when_started(dr, 0, copy.start)

    lane = lax.broadcasted_iota(jnp.int32, (DMAX, cols), 1).astype(F32).astype(BF)
    lane = jnp.concatenate([lane] * (chans // DMAX), axis=0)
    lane_e = lax.broadcasted_iota(jnp.int32, (ext, cols), 1)
    lane_b = lax.broadcasted_iota(jnp.int32, (8, cols), 1)

    def pack_rows(values):
        turns = [values[0]]
        for i in range(1, 8):
            turns.append(pltpu.roll(values[i], 16 * i, 1))
        left, right = turns[7], turns[0]
        for i in range(6, -1, -1):
            inside = lane < 16 * (i + 1)
            left = jnp.where(inside, turns[i], left)
            right = jnp.where(inside, turns[i + 1], right)
        return left, right

    def unpacked(rims, g, i):
        value = jnp.where((lane >= 16 * i) & (lane < 16 * i + 16), rims[1, g], rims[0, g])
        if i:
            value = pltpu.roll(value, cols - 16 * i, 1)
        return value

    d1 = dil[1]
    d0 = dil[0]

    def splat(value):
        return jnp.full((chans, cols), value.astype(F32)).astype(BF)

    def side_shift(tile, halo, index, d):
        if tile.shape[0] == chans:
            where, split = lane, splat(d if index == 0 else cols - d)
        else:
            where, split = lane_e, d if index == 0 else cols - d
        if index == 0:
            return pltpu.roll(jnp.where(where >= split, tile, halo), cols - d, 1)
        return pltpu.roll(jnp.where(where < split, tile, halo), d, 1)

    loads[0].wait()

    @pl.loop(0, 4)
    def _(chunk):
        for half in (0, 1):
            g = 2 * chunk + half
            left, right = pack_rows([pre_e[DMAX + 8 * g + i] for i in range(8)])
            pack[0, g] = left
            pack[1, g] = right

    pl.semaphore_wait(barrier, expected)
    for (dr, dc), copy in early:
        when_started(dr, dc, copy.start)

    loads[1].wait()
    loads[2].wait()
    own = jnp.where(occ[...] > 0, cot[...].astype(F32), 0.0).astype(BF)
    s_own[...] = own
    s_in[1, pl.ds(DMAX, rows)] = own
    s_copies = []
    for k, (dr, dc) in enumerate(AROUND):
        copy = remote(
            s_own.at[pl.ds(*src_rows[dr])],
            s_in.at[1 - dc, pl.ds(*dst_rows[dr])],
            s_send.at[k],
            s_recv.at[k],
            peer(dr, dc),
        )
        s_copies.append(((dr, dc), copy))
        when_started(dr, dc, copy.start)

    loads[3].wait()
    loads[4].wait()
    eye = jnp.where(
        lax.broadcasted_iota(jnp.int32, (chans, chans), 0)
        == lax.broadcasted_iota(jnp.int32, (chans, chans), 1),
        1.0,
        0.0,
    ).astype(F32)
    eye_b = eye.astype(BF)

    def tap(t):
        return w[0, pl.ds(t * chans, chans), :]

    def turned(value):
        return lax.dot_general(eye_b, value, NT, preferred_element_type=F32).astype(BF)

    w1l[...] = turned(w[1])
    c0row = coup[0:1, :].astype(F32)
    c1row = coup[1:2, :].astype(F32)
    c0col = jnp.dot(
        (eye * c0row).astype(BF), jnp.ones((chans, cols), BF), preferred_element_type=F32
    )
    c0col_b = c0col.astype(BF)
    c1rows = jnp.broadcast_to(c1row, (8, chans))
    diag = (
        lax.broadcasted_iota(jnp.int32, (8, 8 * chans), 1) // chans
        == lax.broadcasted_iota(jnp.int32, (8, 8 * chans), 0)
    )
    heads = lax.dot_general(
        c1rows.astype(BF), w[0], NT, preferred_element_type=F32
    )
    for b in range(3):
        w0o[pl.ds(b * chans, chans), :] = turned(
            jnp.concatenate([tap(3 * a + b) for a in range(3)], axis=0)
        )

    def spread(value):
        return jnp.where(diag, jnp.concatenate([value] * 8, axis=1), 0.0)

    vb[...] = jnp.concatenate(
        [spread(heads[:, t * chans : (t + 1) * chans]) for t in range(9)], axis=0
    ).astype(BF)
    cb[...] = jnp.concatenate([spread(c1rows)] * 2, axis=0).astype(BF)
    for t in range(9):
        for start in (DMAX, 2 * DMAX + rows):
            pmap[t, pl.ds(start, DMAX), :] = jnp.zeros((DMAX, cols), F32)
            pmap[t, pl.ds(start - DMAX if start == DMAX else start + DMAX, DMAX), :] = (
                jnp.zeros((DMAX, cols), F32)
            )
    for start in (0, DMAX + rows):
        cmap[pl.ds(start, DMAX), :] = jnp.zeros((DMAX, cols), F32)

    for (dr, dc), copy in early:
        when_expected(dr, dc, copy.wait_recv)

    @pl.loop(0, 3)
    def _(part):
        for quarter in range(4):
            g = part * 4 + quarter
            for i in range(8):
                e = g * 8 + i
                tile = jnp.where(pre_e[e] > 0, c0col_b, 0)
                halo = jnp.where(unpacked(rim, g, i) > 0, c0col_b, 0)
                shifted[e, pl.ds(0, chans), :] = side_shift(tile, halo, 0, d1)
                shifted[e, pl.ds(chans, chans), :] = tile
                shifted[e, pl.ds(2 * chans, chans), :] = side_shift(tile, halo, 2, d1)

    loads[5].wait()

    middle = (level > 0) & (level + 1 < n_level)

    @pl.when(middle)
    def _():
        for t in range(9):
            w1t[t] = turned(w[1, pl.ds(t * chans, chans), :])

        @pl.loop(0, 4)
        def _(chunk):
            keep = [pre0[chunk * 16 + i] > 0 for i in range(16)]
            for t in range(10):
                if t < 9:
                    taps_in = jnp.concatenate(
                        [
                            shifted[
                                chunk * 16 + i + DMAX - (t // 3 - 1) * d1,
                                pl.ds((t % 3) * chans, chans),
                                :,
                            ]
                            for i in range(16)
                        ],
                        axis=1,
                    )
                    made = jnp.dot(w1t[t], taps_in, preferred_element_type=F32).astype(BF)
                    pieces = [made[:, i * cols : (i + 1) * cols] for i in range(16)]
                else:
                    pieces = [c0col_b] * 16
                kept = [jnp.where(keep[i], pieces[i], 0) for i in range(16)]
                for target, lhs, values in ((tmap, vb, kept), (tcen, cb, pieces)):
                    rhs = jnp.concatenate(
                        [
                            jnp.concatenate(values[0:8], axis=0),
                            jnp.concatenate(values[8:16], axis=0),
                        ],
                        axis=1,
                    )
                    maps = jnp.dot(lhs[...], rhs, preferred_element_type=F32)
                    size = target.shape[2]
                    target[t, 2 * chunk] = maps[0:size, 0:cols]
                    target[t, 2 * chunk + 1] = maps[0:size, cols : 2 * cols]

    for (dr, dc), copy in s_copies:
        when_expected(dr, dc, copy.wait_recv)

    q_copies = []
    for k, (dr, dc) in enumerate(NINE):
        if dc == 0:
            src = q_msg.at[pl.ds(*{1: (80, 48), 0: (16, 128), -1: (0, 48)}[dr])]
            dst = in_tile if dr == 0 else in_row.at[(1 - dr) // 2]
        elif dr == 0:
            src = q_side.at[(1 - dc) // 2]
            dst = in_side.at[(1 - dc) // 2]
        else:
            src = q_side.at[(1 - dc) // 2, pl.ds(0, 16)]
            dst = in_corner.at[(1 - dc) // 2, (1 - dr) // 2]
        q_copies.append(((dr, dc), remote(src, dst, q_send.at[k], q_recv.at[k], peer(dr, dc, -1))))

    for (dr, dc), copy in q_copies:

        @pl.when(exists(-dr, -dc) & (level + 1 < n_level))
        def _():
            copy.wait_recv()

    low = lane_e < DMAX
    high = lane_e >= cols - DMAX

    def folded(value):
        found = []
        for j in (0, 2, 1):
            block = value[32 * j : 32 * j + 8]
            block = pltpu.roll(block, DMAX, 1)
            for m in range(1, 4):
                start = 32 * j + 8 * m
                piece = pltpu.roll(value[start : start + 8], (DMAX + 32 * m) % cols, 1)
                block = jnp.where(lane_b // 32 == m, piece, block)
            found.append(block)
        found.append(jnp.zeros((8, cols), F32))
        return jnp.concatenate(found, axis=0).astype(BF)

    def unfolded(block):
        return jnp.concatenate(
            [pltpu.roll(block, (cols - DMAX - 32 * m) % cols, 1) for m in range(4)], axis=0
        )

    def summed(middle, above, below):
        middle, above, below = (part.astype(F32) for part in (middle, above, below))
        return jnp.concatenate(
            [
                unfolded(middle[0:8]) + unfolded(above[8:16]),
                unfolded(middle[16:24]),
                unfolded(middle[8:16]) + unfolded(below[0:8]),
            ],
            axis=0,
        )

    left = summed(in_side[0], in_corner[0, 0], in_corner[0, 1])
    right = summed(in_side[1], in_corner[1, 0], in_corner[1, 1])
    edges = jnp.concatenate(
        [
            in_row[0, pl.ds(0, 32)].astype(F32),
            jnp.zeros((rows - 2 * DMAX, cols), F32),
            in_row[1, pl.ds(16, 32)].astype(F32),
        ],
        axis=0,
    )
    tile = in_tile[pl.ds(0, ext)].astype(F32) + edges + s_in[1].astype(F32)
    tile += jnp.where(low, left, 0.0) + jnp.where(high, right, 0.0)
    halo = summed(in_tile[pl.ds(ext, 32)], in_row[0, pl.ds(32, 16)], in_row[1, pl.ds(0, 16)])
    halo += jnp.where(low, right + s_in[2].astype(F32), left + s_in[0].astype(F32))
    totals[0] = side_shift(tile, halo, 0, d1)
    totals[1] = tile
    totals[2] = side_shift(tile, halo, 2, d1)

    def layer_1(chunk):
        for pair in range(8):
            wide_in = []
            for i in range(2):
                r = chunk * 16 + pair * 2 + i
                parts = []
                for a in (-1, 0, 1):
                    e = r + DMAX - a * d1
                    for b in range(3):
                        line = jnp.broadcast_to(totals[b, pl.ds(e, 1), :], (16, cols)).astype(BF)
                        line = jnp.concatenate([line] * 4, axis=0)
                        parts.append(shifted[e, pl.ds(b * chans, chans), :] * line)
                wide_in.append(jnp.concatenate(parts, axis=0))
            result = jnp.dot(
                w1l[...], jnp.concatenate(wide_in, axis=1), preferred_element_type=F32
            )
            for i in range(2):
                r = chunk * 16 + pair * 2 + i
                value = result[:, i * cols : (i + 1) * cols]
                value += c0col * totals[1, pl.ds(r + DMAX, 1), :]
                grad1[r] = value
                kept = jnp.where(pre0[r] > 0, value.astype(BF), 0)
                m0[r] = kept
                m0_e[r + DMAX] = kept

    def prediction_maps(chunk):
        for half in range(2):
            g = chunk * 2 + half
            first = jnp.concatenate([m0[g * 8 + i] for i in range(8)], axis=0)
            maps = jnp.dot(vb[...], first, preferred_element_type=F32)
            second = jnp.concatenate([grad1[g * 8 + i].astype(BF) for i in range(8)], axis=0)
            center = jnp.dot(cb[...], second, preferred_element_type=F32)
            at = pl.ds(pl.multiple_of(g * 8, 8) + 2 * DMAX, 8)
            for t in range(9):
                pmap[t, at, :] = maps[8 * t : 8 * t + 8]
            cmap[pl.ds(pl.multiple_of(g * 8, 8) + DMAX, 8), :] = center[0:8]

    def column(b):
        found = None
        for a in (-1, 0, 1):
            piece = pmap[(a + 1) * 3 + b + 1, pl.ds(DMAX - a * d0, ext), :]
            found = piece if found is None else found + piece
        return found

    @pl.when(level + 1 == n_level)
    def _():
        @pl.loop(0, 4)
        def _(chunk):
            layer_1(chunk)
            prediction_maps(chunk)

    @pl.when(middle)
    def _():
        @pl.loop(0, 4)
        def _(chunk):
            for half in range(2):
                g = chunk * 2 + half
                lines = [
                    totals[t % 3, pl.ds(g * 8 + DMAX - (t // 3 - 1) * d1, 8), :]
                    for t in range(9)
                ]
                lines.append(totals[1, pl.ds(pl.multiple_of(g * 8, 8) + DMAX, 8), :])
                start = pl.multiple_of(g * 8, 8)
                for k in range(9):
                    found = lines[0] * tmap[0, g, pl.ds(8 * k, 8), :]
                    for t in range(1, 10):
                        found += lines[t] * tmap[t, g, pl.ds(8 * k, 8), :]
                    pmap[k, pl.ds(start + 2 * DMAX, 8), :] = found
                found = lines[0] * tcen[0, g]
                for t in range(1, 10):
                    found += lines[t] * tcen[t, g]
                cmap[pl.ds(start + DMAX, 8), :] = found

    @pl.when(level > 0)
    def _():
        goes_left = pltpu.roll(column(-1), cols - d0, 1)
        goes_right = pltpu.roll(column(1), d0, 1)
        q0 = cmap[...] + column(0)
        q0 += jnp.where(lane_e < cols - d0, goes_left, 0.0)
        q0 += jnp.where(lane_e >= d0, goes_right, 0.0)
        q1 = jnp.where(lane_e >= cols - d0, goes_left, 0.0)
        q1 += jnp.where(lane_e < d0, goes_right, 0.0)
        q_side[0] = folded(jnp.where(low, q1, q0))
        q_side[1] = folded(jnp.where(low, q0, q1))
        rim_part = folded(q1)
        q_msg[pl.ds(0, DMAX)] = rim_part[0:DMAX]
        q_msg[pl.ds(DMAX, ext)] = q0.astype(BF)
        q_msg[pl.ds(DMAX + ext, 32)] = rim_part
        for (dr, dc), copy in q_copies:
            when_started(dr, dc, copy.start)

    @pl.when(level + 1 < n_level)
    def _():
        @pl.loop(0, 4)
        def _(step):
            layer_1(jnp.where(step == 0, 0, jnp.where(step == 1, 3, step - 1)))

            @pl.when(step == 0)
            def _():
                start_late_rows(-1)

            @pl.when(step == 1)
            def _():
                start_late_rows(1)

    @pl.when(level + 1 == n_level)
    def _():
        start_late_rows(-1)
        start_late_rows(1)

    edge = (lane < DMAX) | (lane >= cols - DMAX)
    own_right = lane >= splat(d0)
    own_left = lane < splat(cols - d0)

    def store(chunk):
        span = pl.ds(chunk * 16, 16)
        return pltpu.make_async_copy(out_v.at[span], out.at[span], out_sem.at[chunk])

    def layer_0(chunk, source, offset):
        outer = []
        for pair in range(8):
            wide_in = []
            for i in range(2):
                r = chunk * 16 + pair * 2 + i
                wide_in.append(
                    jnp.concatenate([source[r + offset - a * d0] for a in (-1, 0, 1)], axis=0)
                )
            result = jnp.dot(
                w0o[...], jnp.concatenate(wide_in, axis=1), preferred_element_type=F32
            )
            for i in range(2):
                r = chunk * 16 + pair * 2 + i
                lanes = slice(i * cols, (i + 1) * cols)
                goes_left = pltpu.roll(result[0:chans, lanes].astype(BF), cols - d0, 1)
                goes_right = pltpu.roll(result[2 * chans :, lanes].astype(BF), d0, 1)
                outer.append(jnp.where(own_right, jnp.where(own_left, 0, goes_left), goes_right))
                value = grad1[r] + result[chans : 2 * chans, lanes]
                value += jnp.where(own_left, goes_left, 0).astype(F32)
                value += jnp.where(own_right, goes_right, 0).astype(F32)
                grad1[r] = value
        for half in range(2):
            to_right, to_left = pack_rows(outer[8 * half : 8 * half + 8])
            pack0[0, 2 * chunk + half] = to_left
            pack0[1, 2 * chunk + half] = to_right
        for dc in (1, -1):
            when_started(0, dc, late_side(chunk, dc).start)

    @pl.loop(0, 2)
    def _(step):
        layer_0(step + 1, m0, 0)

    for dr, copy in late_rows:
        when_expected(dr, 0, copy.wait_recv)

    @pl.loop(0, 2)
    def _(step):
        layer_0(step * 3, m0_e, DMAX)

    @pl.loop(0, 4)
    def _(step):
        chunk = jnp.where(step < 2, step + 1, jnp.where(step == 2, 0, 3))
        for dc in (1, -1):
            when_expected(0, dc, late_side(chunk, dc).wait_recv)
        for half in range(2):
            g = chunk * 2 + half
            for i in range(8):
                r = g * 8 + i
                extra = jnp.where(edge, unpacked(rim0, g, i), 0).astype(F32)
                out_v[r] = (grad1[r] + extra).astype(BF)
        store(chunk).start()

    for (dr, dc), copy in early:
        when_started(dr, dc, copy.wait_send)
    for dr, copy in late_rows:
        when_started(dr, 0, copy.wait_send)
    for dc in (1, -1):
        for chunk in range(4):
            when_started(0, dc, late_side(chunk, dc).wait_send)
    for (dr, dc), copy in s_copies:
        when_started(dr, dc, copy.wait_send)

    @pl.when(level > 0)
    def _():
        for (dr, dc), copy in q_copies:
            when_started(dr, dc, copy.wait_send)

    for chunk in range(4):
        store(chunk).wait()


def solution(mesh):
    shape = (mesh.shape["row"], mesh.shape["col"], mesh.shape["level"])

    def on_device(pre_acts, pred_cot, occupancy, conv_weights, coupling, dilation):
        hbm = pl.BlockSpec(memory_space=pl.ANY)
        smem = pl.BlockSpec(memory_space=pltpu.SMEM)
        dma = pltpu.SemaphoreType.DMA
        result = pl.pallas_call(
            functools.partial(kernel, shape),
            out_shape=jax.ShapeDtypeStruct((64, 64, 128), BF),
            in_specs=[smem, hbm, hbm, hbm, hbm, hbm],
            out_specs=hbm,
            scratch_shapes=[
                pltpu.VMEM((64, 128), BF),
                pltpu.VMEM((64, 128), jnp.int32),
                pltpu.VMEM((2, 576, 64), BF),
                pltpu.VMEM((2, 64), BF),
                pltpu.VMEM((96, 64, 128), BF),
                pltpu.VMEM((64, 64, 128), BF),
                pltpu.VMEM((2, 8, 64, 128), BF),
                pltpu.VMEM((2, 12, 64, 128), BF),
                pltpu.VMEM((64, 128), BF),
                pltpu.VMEM((3, 96, 128), BF),
                pltpu.VMEM((96, 192, 128), BF),
                pltpu.VMEM((64, 64, 128), BF),
                pltpu.VMEM((96, 64, 128), BF),
                pltpu.VMEM((2, 8, 64, 128), BF),
                pltpu.VMEM((2, 8, 64, 128), BF),
                pltpu.VMEM((64, 64, 128), F32),
                pltpu.VMEM((3, 96, 128), F32),
                pltpu.VMEM((9, 128, 128), F32),
                pltpu.VMEM((96, 128), F32),
                pltpu.VMEM((144, 128), BF),
                pltpu.VMEM((2, 32, 128), BF),
                pltpu.VMEM((128, 128), BF),
                pltpu.VMEM((2, 32, 128), BF),
                pltpu.VMEM((2, 48, 128), BF),
                pltpu.VMEM((2, 2, 16, 128), BF),
                pltpu.VMEM((64, 576), BF),
                pltpu.VMEM((9, 64, 64), BF),
                pltpu.VMEM((10, 8, 72, 128), F32),
                pltpu.VMEM((10, 8, 8, 128), F32),
                pltpu.VMEM((192, 192), BF),
                pltpu.VMEM((72, 512), BF),
                pltpu.VMEM((16, 512), BF),
                pltpu.VMEM((64, 64, 128), BF),
                dma((6,)),
                dma((4,)),
                dma((20,)),
                dma((20,)),
                dma((8,)),
                dma((8,)),
                dma((9,)),
                dma((9,)),
                dma((16,)),
                dma((16,)),
            ],
            compiler_params=pltpu.CompilerParams(
                collective_id=0, has_side_effects=True, vmem_limit_bytes=64 * 2**20
            ),
        )(
            dilation,
            pre_acts.reshape(2, 64, 64, 128),
            pred_cot.reshape(64, 128),
            occupancy.reshape(64, 128),
            conv_weights.reshape(2, 576, 64),
            coupling.reshape(2, 64),
        )
        return result[None]

    return jax.shard_map(
        on_device,
        mesh=mesh,
        in_specs=(
            P("level", None, "row", None, "col"),
            P("level", "row", "col"),
            P("level", "row", "col"),
            P("level", None, None, None, None, None),
            P("level", None, None),
            P(),
        ),
        out_specs=P("level", "row", None, "col"),
        check_vma=False,
    )
```

```python
import functools

import jax
import jax.numpy as jnp
from jax import lax
from jax.experimental import pallas as pl
from jax.experimental.pallas import tpu as pltpu
from jax.sharding import PartitionSpec as P

MESH = pl.DeviceIdType.MESH
BF = jnp.bfloat16
F32 = jnp.float32
DMAX = 16
AROUND = [(dr, dc) for dr in (-1, 0, 1) for dc in (-1, 0, 1) if (dr, dc) != (0, 0)]
NINE = [(0, 0)] + AROUND
NT = (((1,), (1,)), ((), ()))


def kernel(
    shape,
    dil,
    pre,
    cot_hbm,
    occ_hbm,
    w_hbm,
    coup_hbm,
    out,
    cot,
    occ,
    w,
    coup,
    pre_e,
    pre0,
    pack,
    rim,
    s_own,
    s_in,
    shifted,
    m0_e,
    m0_rows,
    pack_c,
    rim_c,
    outside,
    pack0,
    rim0,
    grad1,
    totals,
    pmap,
    cmap,
    q_msg,
    q_side,
    in_tile,
    in_side,
    in_row,
    in_corner,
    w1l,
    w1t,
    tmap,
    tcen,
    w0o,
    w0r,
    pmat,
    smat,
    umat,
    omat,
    vb,
    cb,
    out_v,
    local_sem,
    out_sem,
    a_send,
    a_recv,
    s_send,
    s_recv,
    q_send,
    q_recv,
    m_send,
    m_recv,
):
    n_row, n_col, n_level = shape
    rows, chans, cols = 64, 64, 128
    ext = rows + 2 * DMAX
    row = lax.axis_index("row")
    col = lax.axis_index("col")
    level = lax.axis_index("level")

    def exists(dr, dc):
        return (
            (row + dr >= 0) & (row + dr < n_row) & (col + dc >= 0) & (col + dc < n_col)
        )

    def peer(dr, dc, dl=0):
        return {"row": row + dr, "col": col + dc, "level": level + dl}

    def remote(src, dst, send, recv, device):
        return pltpu.make_async_remote_copy(
            src_ref=src,
            dst_ref=dst,
            send_sem=send,
            recv_sem=recv,
            device_id=device,
            device_id_type=MESH,
        )

    loads = [
        pltpu.make_async_copy(src, dst, local_sem.at[i])
        for i, (src, dst) in enumerate(
            (
                (pre.at[1], pre_e.at[pl.ds(DMAX, rows)]),
                (cot_hbm, cot),
                (occ_hbm, occ),
                (w_hbm, w),
                (coup_hbm, coup),
                (pre.at[0], pre0),
            )
        )
    ]
    for load in loads:
        load.start()

    for ref in (s_in, in_tile, in_side, in_row, in_corner):
        ref[...] = jnp.zeros_like(ref)

    barrier = pltpu.get_barrier_semaphore()
    for dr, dc in AROUND:

        @pl.when(exists(dr, dc))
        def _():
            pl.semaphore_signal(barrier, inc=1, device_id=peer(dr, dc), device_id_type=MESH)

    for dr, dc in NINE:

        @pl.when(exists(dr, dc) & (level + 1 < n_level))
        def _():
            pl.semaphore_signal(
                barrier, inc=1, device_id=peer(dr, dc, 1), device_id_type=MESH
            )

    count_r = jnp.where(row > 0, 1, 0) + 1 + jnp.where(row + 1 < n_row, 1, 0)
    count_c = jnp.where(col > 0, 1, 0) + 1 + jnp.where(col + 1 < n_col, 1, 0)
    around = count_r * count_c
    expected = around - 1 + jnp.where(level > 0, around, 0)

    for side, cond in ((0, row == 0), (1, row + 1 == n_row)):

        @pl.when(cond)
        def _():
            span = pl.ds(0 if side == 0 else DMAX + rows, DMAX)
            pre_e[span] = jnp.zeros((DMAX, chans, cols), BF)
            m0_rows[side] = jnp.zeros((DMAX, chans, cols), BF)
            groups = pl.ds(0 if side == 0 else 10, 2)
            for lr in (0, 1):
                rim[lr, groups] = jnp.zeros((2, chans, cols), BF)
                rim_c[lr, pl.ds(2 * side, 2)] = jnp.zeros((2, chans, cols), BF)

    for side, cond in ((0, col == 0), (1, col + 1 == n_col)):

        @pl.when(cond)
        def _():
            rim[side] = jnp.zeros((12, chans, cols), BF)
            rim_c[side] = jnp.zeros((4, chans, cols), BF)
            rim0[1 - side] = jnp.zeros((8, chans, cols), BF)

    src_rows = {1: (48, 16), 0: (0, 64), -1: (0, 16)}
    dst_rows = {1: (0, 16), 0: (16, 64), -1: (80, 16)}

    def row_copies(source, targets, send, recv):
        found = []
        for dr in (1, -1):
            for part in range(4):
                k = 4 * ((1 - dr) // 2) + part
                copy = remote(
                    source.at[pl.ds(src_rows[dr][0] + 4 * part, 4)],
                    targets[dr].at[pl.ds(4 * part, 4)],
                    send.at[k],
                    recv.at[k],
                    peer(dr, 0),
                )
                found.append((dr, copy))
        return found

    def corner_copy(packed, rims, send, recv, dr, dc):
        k = 8 + (1 - dr) + (1 - dc) // 2
        return remote(
            packed.at[(1 + dc) // 2, pl.ds(6 if dr == 1 else 0, 2)],
            rims.at[(1 - dc) // 2, pl.ds(0 if dr == 1 else 10, 2)],
            send.at[k],
            recv.at[k],
            peer(dr, dc),
        )

    def side_copy(packed, rims, send, recv, dc, chunk):
        k = 12 + 4 * ((1 - dc) // 2) + chunk
        return remote(
            packed.at[(1 + dc) // 2, pl.ds(2 * chunk, 2)],
            rims.at[(1 - dc) // 2, pl.ds(2 * chunk + 2, 2)],
            send.at[k],
            recv.at[k],
            peer(0, dc),
        )

    def when_started(dr, dc, act):
        @pl.when(exists(dr, dc))
        def _():
            act()

    def when_expected(dr, dc, act):
        @pl.when(exists(-dr, -dc))
        def _():
            act()

    early = [((dr, 0), copy) for dr, copy in row_copies(
        pre.at[1],
        {dr: pre_e.at[pl.ds(*dst_rows[dr])] for dr in (1, -1)},
        a_send,
        a_recv,
    )]
    for chunk in range(4):
        for dc in (1, -1):
            early.append(((0, dc), side_copy(pack, rim, a_send, a_recv, dc, chunk)))
    for dr in (1, -1):
        for dc in (1, -1):
            early.append(((dr, dc), corner_copy(pack, rim, a_send, a_recv, dr, dc)))
    late_rows = row_copies(
        m0_e.at[pl.ds(DMAX, rows)], {1: m0_rows.at[0], -1: m0_rows.at[1]}, m_send, m_recv
    )
    late_corners = []
    for dr in (1, -1):
        for dc in (1, -1):
            k = 16 + (1 - dr) + (1 - dc) // 2
            copy = remote(
                pack_c.at[(1 + dc) // 2, pl.ds(2 if dr == 1 else 0, 2)],
                rim_c.at[(1 - dc) // 2, pl.ds(0 if dr == 1 else 2, 2)],
                m_send.at[k],
                m_recv.at[k],
                peer(dr, dc),
            )
            late_corners.append(((dr, dc), copy))

    def late_side(chunk, dc):
        k = 8 + 4 * ((1 - dc) // 2) + chunk
        return remote(
            pack0.at[(1 + dc) // 2, pl.ds(2 * chunk, 2)],
            rim0.at[(1 + dc) // 2, pl.ds(2 * chunk, 2)],
            m_send.at[k],
            m_recv.at[k],
            peer(0, dc),
        )

    lane = lax.broadcasted_iota(jnp.int32, (DMAX, cols), 1).astype(F32).astype(BF)
    lane = jnp.concatenate([lane] * (chans // DMAX), axis=0)
    lane_e = lax.broadcasted_iota(jnp.int32, (ext, cols), 1)
    lane_b = lax.broadcasted_iota(jnp.int32, (8, cols), 1)

    def picks(size, *wanted):
        k = lax.broadcasted_iota(jnp.int32, (size, wanted[0].shape[1]), 0)
        found = k == wanted[0]
        for other in wanted[1:]:
            found = found | (k == other)
        return jnp.where(found, 1.0, 0.0).astype(BF)

    n_wide = lax.broadcasted_iota(jnp.int32, (1, 2 * cols), 1)
    n_one = lax.broadcasted_iota(jnp.int32, (1, cols), 1)
    w_wide = jnp.where(n_wide < cols, n_wide, n_wide - cols)
    group = w_wide // 16
    inner = w_wide % 16
    pmat[...] = picks(
        8 * cols,
        jnp.where(
            n_wide < cols,
            group * cols + inner,
            ((group + 1) % 8) * cols + cols - DMAX + inner,
        ),
    )

    def pack_rows(values):
        both = jnp.dot(
            jnp.concatenate(values, axis=1), pmat[...], preferred_element_type=F32
        ).astype(BF)
        return both[:, 0:cols], both[:, cols:]

    def send_outer(which):
        for dr, copy in late_rows:
            if dr == which:
                when_started(dr, 0, copy.start)
        for half in (0, 1):
            g = half + (6 if which == 1 else 0)
            left, right = pack_rows([m0_e[DMAX + 8 * g + i] for i in range(8)])
            slot = half + (2 if which == 1 else 0)
            pack_c[0, slot] = left
            pack_c[1, slot] = right
        for (dr, dc), copy in late_corners:
            if dr == which:
                when_started(dr, dc, copy.start)

    def merged(rims, g, i):
        return jnp.where((lane >= 16 * i) & (lane < 16 * i + 16), rims[1, g], rims[0, g])

    d1 = dil[1]
    d0 = dil[0]

    def side_shift(tile, halo, index, d):
        where, split = lane_e, d if index == 0 else cols - d
        if index == 0:
            return pltpu.roll(jnp.where(where >= split, tile, halo), cols - d, 1)
        return pltpu.roll(jnp.where(where < split, tile, halo), d, 1)

    loads[0].wait()

    @pl.loop(0, 4)
    def _(chunk):
        for half in (0, 1):
            g = 2 * chunk + half
            left, right = pack_rows([pre_e[DMAX + 8 * g + i] for i in range(8)])
            pack[0, g] = left
            pack[1, g] = right

    pl.semaphore_wait(barrier, expected)
    for (dr, dc), copy in early:
        when_started(dr, dc, copy.start)

    loads[1].wait()
    loads[2].wait()
    own = jnp.where(occ[...] > 0, cot[...].astype(F32), 0.0).astype(BF)
    s_own[...] = own
    s_in[1, pl.ds(DMAX, rows)] = own
    s_copies = []
    for k, (dr, dc) in enumerate(AROUND):
        copy = remote(
            s_own.at[pl.ds(*src_rows[dr])],
            s_in.at[1 - dc, pl.ds(*dst_rows[dr])],
            s_send.at[k],
            s_recv.at[k],
            peer(dr, dc),
        )
        s_copies.append(((dr, dc), copy))
        when_started(dr, dc, copy.start)

    loads[3].wait()
    loads[4].wait()
    eye = jnp.where(
        lax.broadcasted_iota(jnp.int32, (chans, chans), 0)
        == lax.broadcasted_iota(jnp.int32, (chans, chans), 1),
        1.0,
        0.0,
    ).astype(F32)
    eye_b = eye.astype(BF)

    def tap(t):
        return w[0, pl.ds(t * chans, chans), :]

    def turned(value):
        return lax.dot_general(eye_b, value, NT, preferred_element_type=F32).astype(BF)

    w1l[...] = turned(w[1])
    c0row = coup[0:1, :].astype(F32)
    c1row = coup[1:2, :].astype(F32)
    c0col = jnp.dot(
        (eye * c0row).astype(BF), jnp.ones((chans, cols), BF), preferred_element_type=F32
    )
    c0col_b = c0col.astype(BF)
    c1rows = jnp.broadcast_to(c1row, (8, chans))
    diag = (
        lax.broadcasted_iota(jnp.int32, (8, 8 * chans), 1) // chans
        == lax.broadcasted_iota(jnp.int32, (8, 8 * chans), 0)
    )
    heads = lax.dot_general(
        c1rows.astype(BF), w[0], NT, preferred_element_type=F32
    )
    for b in range(3):
        w0o[pl.ds(b * chans, chans), :] = turned(
            jnp.concatenate([tap(3 * a + b) for a in range(3)], axis=0)
        )

    for layer, d in ((1, d1), (0, d0)):
        right = n_wide + d
        left = w_wide - d
        for i in range(8):
            smat[layer, i] = picks(
                2 * cols,
                jnp.where(
                    n_wide < cols,
                    jnp.where(right < cols, right, right + 16 * i),
                    jnp.where(left >= 0, left, cols + ((left + 16 * i + cols) % cols)),
                ),
            )
    for i in range(8):
        umat[i] = picks(
            cols,
            jnp.where(
                n_one < DMAX,
                n_one + 16 * i,
                jnp.where(n_one >= cols - DMAX, (n_one + 16 * i) % cols, -1),
            ),
        )
    omat[...] = picks(
        2 * cols,
        jnp.where(
            n_wide < cols,
            jnp.where(w_wide + d0 < cols, w_wide + d0, -1),
            jnp.where(w_wide >= cols - d0, w_wide + d0 - cols, -1),
        ),
        jnp.where(
            n_wide < cols,
            jnp.where(w_wide >= d0, cols + w_wide - d0, -1),
            jnp.where(w_wide < d0, 2 * cols + w_wide - d0, -1),
        ),
    )
    w0r[0] = turned(w[0, pl.ds(6 * chans, 3 * chans), :])
    w0r[1] = turned(w[0, pl.ds(0, 3 * chans), :])
    for side in (0, 1):
        m0_e[pl.ds(side * (DMAX + rows), DMAX)] = jnp.zeros((DMAX, chans, cols), BF)
        outside[side, pl.ds(16 - 16 * side, 16)] = jnp.zeros((DMAX, 3 * chans, cols), BF)

    def spread(value):
        return jnp.where(diag, jnp.concatenate([value] * 8, axis=1), 0.0)

    vb[...] = jnp.concatenate(
        [spread(heads[:, t * chans : (t + 1) * chans]) for t in range(9)], axis=0
    ).astype(BF)
    cb[...] = jnp.concatenate([spread(c1rows)] * 2, axis=0).astype(BF)
    for t in range(9):
        for start in (DMAX, 2 * DMAX + rows):
            pmap[t, pl.ds(start, DMAX), :] = jnp.zeros((DMAX, cols), F32)
            pmap[t, pl.ds(start - DMAX if start == DMAX else start + DMAX, DMAX), :] = (
                jnp.zeros((DMAX, cols), F32)
            )
    for start in (0, DMAX + rows):
        cmap[pl.ds(start, DMAX), :] = jnp.zeros((DMAX, cols), F32)

    for (dr, dc), copy in early:
        when_expected(dr, dc, copy.wait_recv)

    @pl.loop(0, 3)
    def _(part):
        for i in range(8):
            wide_in = []
            for quarter in range(4):
                g = part * 4 + quarter
                e = g * 8 + i
                tile = jnp.where(pre_e[e] > 0, c0col_b, 0)
                halo = jnp.where(merged(rim, g, i) > 0, c0col_b, 0)
                shifted[e, pl.ds(chans, chans), :] = tile
                wide_in.append(jnp.concatenate([tile, halo], axis=1))
            both = jnp.dot(
                jnp.concatenate(wide_in, axis=0), smat[1, i], preferred_element_type=F32
            ).astype(BF)
            for quarter in range(4):
                e = (part * 4 + quarter) * 8 + i
                here = both[quarter * chans : (quarter + 1) * chans]
                shifted[e, pl.ds(0, chans), :] = here[:, 0:cols]
                shifted[e, pl.ds(2 * chans, chans), :] = here[:, cols:]

    loads[5].wait()

    middle = (level > 0) & (level + 1 < n_level)

    @pl.when(middle)
    def _():
        for t in range(9):
            w1t[t] = turned(w[1, pl.ds(t * chans, chans), :])

        @pl.loop(0, 4)
        def _(chunk):
            keep = [pre0[chunk * 16 + i] > 0 for i in range(16)]
            for t in range(10):
                if t < 9:
                    taps_in = jnp.concatenate(
                        [
                            shifted[
                                chunk * 16 + i + DMAX - (t // 3 - 1) * d1,
                                pl.ds((t % 3) * chans, chans),
                                :,
                            ]
                            for i in range(16)
                        ],
                        axis=1,
                    )
                    made = jnp.dot(w1t[t], taps_in, preferred_element_type=F32).astype(BF)
                    pieces = [made[:, i * cols : (i + 1) * cols] for i in range(16)]
                else:
                    pieces = [c0col_b] * 16
                kept = [jnp.where(keep[i], pieces[i], 0) for i in range(16)]
                for target, lhs, values in ((tmap, vb, kept), (tcen, cb, pieces)):
                    rhs = jnp.concatenate(
                        [
                            jnp.concatenate(values[0:8], axis=0),
                            jnp.concatenate(values[8:16], axis=0),
                        ],
                        axis=1,
                    )
                    maps = jnp.dot(lhs[...], rhs, preferred_element_type=F32)
                    size = target.shape[2]
                    target[t, 2 * chunk] = maps[0:size, 0:cols]
                    target[t, 2 * chunk + 1] = maps[0:size, cols : 2 * cols]

    for (dr, dc), copy in s_copies:
        when_expected(dr, dc, copy.wait_recv)

    q_copies = []
    for k, (dr, dc) in enumerate(NINE):
        if dc == 0:
            src = q_msg.at[pl.ds(*{1: (80, 48), 0: (16, 128), -1: (0, 48)}[dr])]
            dst = in_tile if dr == 0 else in_row.at[(1 - dr) // 2]
        elif dr == 0:
            src = q_side.at[(1 - dc) // 2]
            dst = in_side.at[(1 - dc) // 2]
        else:
            src = q_side.at[(1 - dc) // 2, pl.ds(0, 16)]
            dst = in_corner.at[(1 - dc) // 2, (1 - dr) // 2]
        q_copies.append(((dr, dc), remote(src, dst, q_send.at[k], q_recv.at[k], peer(dr, dc, -1))))

    for (dr, dc), copy in q_copies:

        @pl.when(exists(-dr, -dc) & (level + 1 < n_level))
        def _():
            copy.wait_recv()

    low = lane_e < DMAX
    high = lane_e >= cols - DMAX

    def folded(value):
        found = []
        for j in (0, 2, 1):
            block = value[32 * j : 32 * j + 8]
            block = pltpu.roll(block, DMAX, 1)
            for m in range(1, 4):
                start = 32 * j + 8 * m
                piece = pltpu.roll(value[start : start + 8], (DMAX + 32 * m) % cols, 1)
                block = jnp.where(lane_b // 32 == m, piece, block)
            found.append(block)
        found.append(jnp.zeros((8, cols), F32))
        return jnp.concatenate(found, axis=0).astype(BF)

    def unfolded(block):
        return jnp.concatenate(
            [pltpu.roll(block, (cols - DMAX - 32 * m) % cols, 1) for m in range(4)], axis=0
        )

    def summed(middle, above, below):
        middle, above, below = (part.astype(F32) for part in (middle, above, below))
        return jnp.concatenate(
            [
                unfolded(middle[0:8]) + unfolded(above[8:16]),
                unfolded(middle[16:24]),
                unfolded(middle[8:16]) + unfolded(below[0:8]),
            ],
            axis=0,
        )

    left = summed(in_side[0], in_corner[0, 0], in_corner[0, 1])
    right = summed(in_side[1], in_corner[1, 0], in_corner[1, 1])
    edges = jnp.concatenate(
        [
            in_row[0, pl.ds(0, 32)].astype(F32),
            jnp.zeros((rows - 2 * DMAX, cols), F32),
            in_row[1, pl.ds(16, 32)].astype(F32),
        ],
        axis=0,
    )
    tile = in_tile[pl.ds(0, ext)].astype(F32) + edges + s_in[1].astype(F32)
    tile += jnp.where(low, left, 0.0) + jnp.where(high, right, 0.0)
    halo = summed(in_tile[pl.ds(ext, 32)], in_row[0, pl.ds(32, 16)], in_row[1, pl.ds(0, 16)])
    halo += jnp.where(low, right + s_in[2].astype(F32), left + s_in[0].astype(F32))
    totals[0] = side_shift(tile, halo, 0, d1)
    totals[1] = tile
    totals[2] = side_shift(tile, halo, 2, d1)

    def layer_1(chunk):
        for pair in range(8):
            wide_in = []
            for i in range(2):
                r = chunk * 16 + pair * 2 + i
                parts = []
                for a in (-1, 0, 1):
                    e = r + DMAX - a * d1
                    for b in range(3):
                        line = jnp.broadcast_to(totals[b, pl.ds(e, 1), :], (16, cols)).astype(BF)
                        line = jnp.concatenate([line] * 4, axis=0)
                        parts.append(shifted[e, pl.ds(b * chans, chans), :] * line)
                wide_in.append(jnp.concatenate(parts, axis=0))
            result = jnp.dot(
                w1l[...], jnp.concatenate(wide_in, axis=1), preferred_element_type=F32
            )
            for i in range(2):
                r = chunk * 16 + pair * 2 + i
                value = result[:, i * cols : (i + 1) * cols]
                value += c0col * totals[1, pl.ds(r + DMAX, 1), :]
                grad1[r] = value
                kept = jnp.where(pre0[r] > 0, value.astype(BF), 0)
                m0_e[r + DMAX] = kept

    def prediction_maps(chunk):
        for half in range(2):
            g = chunk * 2 + half
            first = jnp.concatenate([m0_e[DMAX + g * 8 + i] for i in range(8)], axis=0)
            maps = jnp.dot(vb[...], first, preferred_element_type=F32)
            second = jnp.concatenate([grad1[g * 8 + i].astype(BF) for i in range(8)], axis=0)
            center = jnp.dot(cb[...], second, preferred_element_type=F32)
            at = pl.ds(pl.multiple_of(g * 8, 8) + 2 * DMAX, 8)
            for t in range(9):
                pmap[t, at, :] = maps[8 * t : 8 * t + 8]
            cmap[pl.ds(pl.multiple_of(g * 8, 8) + DMAX, 8), :] = center[0:8]

    def column(b):
        found = None
        for a in (-1, 0, 1):
            piece = pmap[(a + 1) * 3 + b + 1, pl.ds(DMAX - a * d0, ext), :]
            found = piece if found is None else found + piece
        return found

    @pl.when(level + 1 == n_level)
    def _():
        @pl.loop(0, 4)
        def _(chunk):
            layer_1(chunk)
            prediction_maps(chunk)

    @pl.when(middle)
    def _():
        @pl.loop(0, 4)
        def _(chunk):
            for half in range(2):
                g = chunk * 2 + half
                lines = [
                    totals[t % 3, pl.ds(g * 8 + DMAX - (t // 3 - 1) * d1, 8), :]
                    for t in range(9)
                ]
                lines.append(totals[1, pl.ds(pl.multiple_of(g * 8, 8) + DMAX, 8), :])
                start = pl.multiple_of(g * 8, 8)
                for k in range(9):
                    found = lines[0] * tmap[0, g, pl.ds(8 * k, 8), :]
                    for t in range(1, 10):
                        found += lines[t] * tmap[t, g, pl.ds(8 * k, 8), :]
                    pmap[k, pl.ds(start + 2 * DMAX, 8), :] = found
                found = lines[0] * tcen[0, g]
                for t in range(1, 10):
                    found += lines[t] * tcen[t, g]
                cmap[pl.ds(start + DMAX, 8), :] = found

    @pl.when(level > 0)
    def _():
        goes_left = pltpu.roll(column(-1), cols - d0, 1)
        goes_right = pltpu.roll(column(1), d0, 1)
        q0 = cmap[...] + column(0)
        q0 += jnp.where(lane_e < cols - d0, goes_left, 0.0)
        q0 += jnp.where(lane_e >= d0, goes_right, 0.0)
        q1 = jnp.where(lane_e >= cols - d0, goes_left, 0.0)
        q1 += jnp.where(lane_e < d0, goes_right, 0.0)
        q_side[0] = folded(jnp.where(low, q1, q0))
        q_side[1] = folded(jnp.where(low, q0, q1))
        rim_part = folded(q1)
        q_msg[pl.ds(0, DMAX)] = rim_part[0:DMAX]
        q_msg[pl.ds(DMAX, ext)] = q0.astype(BF)
        q_msg[pl.ds(DMAX + ext, 32)] = rim_part
        for (dr, dc), copy in q_copies:
            when_started(dr, dc, copy.start)

    @pl.when(level + 1 < n_level)
    def _():
        @pl.loop(0, 4)
        def _(step):
            layer_1(jnp.where(step == 0, 0, jnp.where(step == 1, 3, step - 1)))

            @pl.when(step == 0)
            def _():
                send_outer(-1)

            @pl.when(step == 1)
            def _():
                send_outer(1)

    @pl.when(level + 1 == n_level)
    def _():
        send_outer(-1)
        send_outer(1)

    def store(chunk):
        span = pl.ds(chunk * 16, 16)
        return pltpu.make_async_copy(out_v.at[span], out.at[span], out_sem.at[chunk])

    @pl.loop(0, 4)
    def _(chunk):
        outer = []
        for pair in range(8):
            wide_in = []
            for i in range(2):
                r = chunk * 16 + pair * 2 + i
                wide_in.append(
                    jnp.concatenate([m0_e[r + DMAX - a * d0] for a in (-1, 0, 1)], axis=0)
                )
            result = jnp.dot(
                w0o[...], jnp.concatenate(wide_in, axis=1), preferred_element_type=F32
            )
            moved = jnp.dot(
                jnp.concatenate(
                    [
                        jnp.concatenate(
                            [
                                result[0:chans, i * cols : (i + 1) * cols],
                                result[2 * chans :, i * cols : (i + 1) * cols],
                            ],
                            axis=1,
                        )
                        for i in range(2)
                    ],
                    axis=0,
                ).astype(BF),
                omat[...],
                preferred_element_type=F32,
            )
            for i in range(2):
                r = chunk * 16 + pair * 2 + i
                here = moved[i * chans : (i + 1) * chans]
                outer.append(here[:, cols:].astype(BF))
                grad1[r] = (
                    grad1[r] + result[chans : 2 * chans, i * cols : (i + 1) * cols] + here[:, 0:cols]
                )
        for half in range(2):
            to_right, to_left = pack_rows(outer[8 * half : 8 * half + 8])
            pack0[0, 2 * chunk + half] = to_left
            pack0[1, 2 * chunk + half] = to_right
        for dc in (1, -1):
            when_started(0, dc, late_side(chunk, dc).start)

    def finish(chunk, more):
        for dc in (1, -1):
            when_expected(0, dc, late_side(chunk, dc).wait_recv)
        for i in range(8):
            extra = jnp.dot(
                jnp.concatenate([merged(rim0, chunk * 2 + half, i) for half in range(2)], axis=0),
                umat[i],
                preferred_element_type=F32,
            )
            for half in range(2):
                r = chunk * 16 + half * 8 + i
                value = grad1[r] + extra[half * chans : (half + 1) * chans]
                if more is not None:
                    value += more[8 * half + i]
                out_v[r] = value.astype(BF)
        store(chunk).start()

    @pl.loop(1, 3)
    def _(chunk):
        finish(chunk, None)

    for dr, copy in late_rows:
        when_expected(dr, 0, copy.wait_recv)
    for (dr, dc), copy in late_corners:
        when_expected(dr, dc, copy.wait_recv)

    @pl.loop(0, 2)
    def _(side):
        for i in range(8):
            wide_in = []
            for half in range(2):
                tile = m0_rows[side, 8 * half + i]
                halo = merged(rim_c, 2 * side + half, i)
                outside[side, 16 * side + 8 * half + i, pl.ds(chans, chans), :] = tile
                wide_in.append(jnp.concatenate([tile, halo], axis=1))
            both = jnp.dot(
                jnp.concatenate(wide_in, axis=0), smat[0, i], preferred_element_type=F32
            ).astype(BF)
            for half in range(2):
                e = 16 * side + 8 * half + i
                here = both[half * chans : (half + 1) * chans]
                outside[side, e, pl.ds(0, chans), :] = here[:, 0:cols]
                outside[side, e, pl.ds(2 * chans, chans), :] = here[:, cols:]

    @pl.loop(0, 2)
    def _(side):
        first = jnp.where(side == 0, DMAX - d0, d0)
        more = []
        for pair in range(8):
            wide_in = [outside[side, first + pair * 2 + i] for i in range(2)]
            result = jnp.dot(
                w0r[side], jnp.concatenate(wide_in, axis=1), preferred_element_type=F32
            )
            more += [result[:, i * cols : (i + 1) * cols] for i in range(2)]
        finish(3 * side, more)

    for (dr, dc), copy in early:
        when_started(dr, dc, copy.wait_send)
    for dr, copy in late_rows:
        when_started(dr, 0, copy.wait_send)
    for (dr, dc), copy in late_corners:
        when_started(dr, dc, copy.wait_send)
    for dc in (1, -1):
        for chunk in range(4):
            when_started(0, dc, late_side(chunk, dc).wait_send)
    for (dr, dc), copy in s_copies:
        when_started(dr, dc, copy.wait_send)

    @pl.when(level > 0)
    def _():
        for (dr, dc), copy in q_copies:
            when_started(dr, dc, copy.wait_send)

    for chunk in range(4):
        store(chunk).wait()


def hand_over(source, target):
    target[...] = source[...]


def solution(mesh):
    shape = (mesh.shape["row"], mesh.shape["col"], mesh.shape["level"])

    def on_device(pre_acts, pred_cot, occupancy, conv_weights, coupling, dilation):
        hbm = pl.BlockSpec(memory_space=pl.ANY)
        smem = pl.BlockSpec(memory_space=pltpu.SMEM)
        dma = pltpu.SemaphoreType.DMA
        result = pl.pallas_call(
            functools.partial(kernel, shape),
            out_shape=jax.ShapeDtypeStruct((64, 64, 128), BF),
            in_specs=[smem, hbm, hbm, hbm, hbm, hbm],
            out_specs=hbm,
            scratch_shapes=[
                pltpu.VMEM((64, 128), BF),
                pltpu.VMEM((64, 128), jnp.int32),
                pltpu.VMEM((2, 576, 64), BF),
                pltpu.VMEM((2, 64), BF),
                pltpu.VMEM((96, 64, 128), BF),
                pltpu.VMEM((64, 64, 128), BF),
                pltpu.VMEM((2, 8, 64, 128), BF),
                pltpu.VMEM((2, 12, 64, 128), BF),
                pltpu.VMEM((64, 128), BF),
                pltpu.VMEM((3, 96, 128), BF),
                pltpu.VMEM((96, 192, 128), BF),
                pltpu.VMEM((96, 64, 128), BF),
                pltpu.VMEM((2, 16, 64, 128), BF),
                pltpu.VMEM((2, 4, 64, 128), BF),
                pltpu.VMEM((2, 4, 64, 128), BF),
                pltpu.VMEM((2, 32, 192, 128), BF),
                pltpu.VMEM((2, 8, 64, 128), BF),
                pltpu.VMEM((2, 8, 64, 128), BF),
                pltpu.VMEM((64, 64, 128), F32),
                pltpu.VMEM((3, 96, 128), F32),
                pltpu.VMEM((9, 128, 128), F32),
                pltpu.VMEM((96, 128), F32),
                pltpu.VMEM((144, 128), BF),
                pltpu.VMEM((2, 32, 128), BF),
                pltpu.VMEM((128, 128), BF),
                pltpu.VMEM((2, 32, 128), BF),
                pltpu.VMEM((2, 48, 128), BF),
                pltpu.VMEM((2, 2, 16, 128), BF),
                pltpu.VMEM((64, 576), BF),
                pltpu.VMEM((9, 64, 64), BF),
                pltpu.VMEM((10, 8, 72, 128), F32),
                pltpu.VMEM((10, 8, 8, 128), F32),
                pltpu.VMEM((192, 192), BF),
                pltpu.VMEM((2, 64, 192), BF),
                pltpu.VMEM((1024, 256), BF),
                pltpu.VMEM((2, 8, 256, 256), BF),
                pltpu.VMEM((8, 128, 128), BF),
                pltpu.VMEM((256, 256), BF),
                pltpu.VMEM((72, 512), BF),
                pltpu.VMEM((16, 512), BF),
                pltpu.VMEM((64, 64, 128), BF),
                dma((6,)),
                dma((4,)),
                dma((20,)),
                dma((20,)),
                dma((8,)),
                dma((8,)),
                dma((9,)),
                dma((9,)),
                dma((20,)),
                dma((20,)),
            ],
            compiler_params=pltpu.CompilerParams(
                collective_id=0, has_side_effects=True, vmem_limit_bytes=64 * 2**20
            ),
        )(
            dilation,
            pre_acts.reshape(2, 64, 64, 128),
            pred_cot.reshape(64, 128),
            occupancy.reshape(64, 128),
            conv_weights.reshape(2, 576, 64),
            coupling.reshape(2, 64),
        )
        result = pl.pallas_call(
            hand_over,
            out_shape=jax.ShapeDtypeStruct((64, 64, 128), BF),
            grid=(4,),
            in_specs=[pl.BlockSpec((16, 64, 128), lambda i: (i, 0, 0))],
            out_specs=pl.BlockSpec((16, 64, 128), lambda i: (i, 0, 0)),
            compiler_params=pltpu.CompilerParams(vmem_limit_bytes=64 * 2**20),
        )(result)
        return result[None]

    return jax.shard_map(
        on_device,
        mesh=mesh,
        in_specs=(
            P("level", None, "row", None, "col"),
            P("level", "row", "col"),
            P("level", "row", "col"),
            P("level", None, None, None, None, None),
            P("level", None, None),
            P(),
        ),
        out_specs=P("level", "row", None, "col"),
        check_vma=False,
    )
```

```python
import functools

import jax
import jax.numpy as jnp
from jax import lax
from jax.experimental import pallas as pl
from jax.experimental.pallas import tpu as pltpu
from jax.sharding import PartitionSpec as P

MESH = pl.DeviceIdType.MESH
BF = jnp.bfloat16
F32 = jnp.float32
DMAX = 16
AROUND = [(dr, dc) for dr in (-1, 0, 1) for dc in (-1, 0, 1) if (dr, dc) != (0, 0)]
NINE = [(0, 0)] + AROUND
NT = (((1,), (1,)), ((), ()))


def kernel(
    shape,
    dil,
    pre,
    cot_hbm,
    occ_hbm,
    w_hbm,
    coup_hbm,
    out,
    cot,
    occ,
    w,
    coup,
    pre_e,
    pre0,
    pack,
    rim,
    s_own,
    s_in,
    shifted,
    m0_e,
    m0_rows,
    pack_c,
    rim_c,
    outside,
    pack0,
    rim0,
    grad1,
    totals,
    pmap,
    cmap,
    q_msg,
    q_side,
    in_tile,
    in_side,
    in_row,
    in_corner,
    w1l,
    w1t,
    tmap,
    tcen,
    w0o,
    w0r,
    pmat,
    smat,
    umat,
    omat,
    vb,
    cb,
    out_v,
    local_sem,
    out_sem,
    a_send,
    a_recv,
    s_send,
    s_recv,
    q_send,
    q_recv,
    m_send,
    m_recv,
):
    n_row, n_col, n_level = shape
    rows, chans, cols = 64, 64, 128
    ext = rows + 2 * DMAX
    row = lax.axis_index("row")
    col = lax.axis_index("col")
    level = lax.axis_index("level")

    def exists(dr, dc):
        return (
            (row + dr >= 0) & (row + dr < n_row) & (col + dc >= 0) & (col + dc < n_col)
        )

    def peer(dr, dc, dl=0):
        return {"row": row + dr, "col": col + dc, "level": level + dl}

    def remote(src, dst, send, recv, device):
        return pltpu.make_async_remote_copy(
            src_ref=src,
            dst_ref=dst,
            send_sem=send,
            recv_sem=recv,
            device_id=device,
            device_id_type=MESH,
        )

    loads = [
        pltpu.make_async_copy(src, dst, local_sem.at[i])
        for i, (src, dst) in enumerate(
            (
                (pre.at[1], pre_e.at[pl.ds(DMAX, rows)]),
                (cot_hbm, cot),
                (occ_hbm, occ),
                (w_hbm, w),
                (coup_hbm, coup),
                (pre.at[0], pre0),
            )
        )
    ]
    for load in loads:
        load.start()

    for ref in (s_in, in_tile, in_side, in_row, in_corner):
        ref[...] = jnp.zeros_like(ref)

    barrier = pltpu.get_barrier_semaphore()
    for dr, dc in AROUND:

        @pl.when(exists(dr, dc))
        def _():
            pl.semaphore_signal(barrier, inc=1, device_id=peer(dr, dc), device_id_type=MESH)

    for dr, dc in NINE:

        @pl.when(exists(dr, dc) & (level + 1 < n_level))
        def _():
            pl.semaphore_signal(
                barrier, inc=1, device_id=peer(dr, dc, 1), device_id_type=MESH
            )

    count_r = jnp.where(row > 0, 1, 0) + 1 + jnp.where(row + 1 < n_row, 1, 0)
    count_c = jnp.where(col > 0, 1, 0) + 1 + jnp.where(col + 1 < n_col, 1, 0)
    around = count_r * count_c
    expected = around - 1 + jnp.where(level > 0, around, 0)

    for side, cond in ((0, row == 0), (1, row + 1 == n_row)):

        @pl.when(cond)
        def _():
            span = pl.ds(0 if side == 0 else DMAX + rows, DMAX)
            pre_e[span] = jnp.zeros((DMAX, chans, cols), BF)
            m0_rows[side] = jnp.zeros((DMAX, chans, cols), BF)
            groups = pl.ds(0 if side == 0 else 10, 2)
            for lr in (0, 1):
                rim[lr, groups] = jnp.zeros((2, chans, cols), BF)
                rim_c[lr, pl.ds(2 * side, 2)] = jnp.zeros((2, chans, cols), BF)

    for side, cond in ((0, col == 0), (1, col + 1 == n_col)):

        @pl.when(cond)
        def _():
            rim[side] = jnp.zeros((12, chans, cols), BF)
            rim_c[side] = jnp.zeros((4, chans, cols), BF)
            rim0[1 - side] = jnp.zeros((8, chans, cols), BF)

    src_rows = {1: (48, 16), 0: (0, 64), -1: (0, 16)}
    dst_rows = {1: (0, 16), 0: (16, 64), -1: (80, 16)}

    def row_copies(source, targets, send, recv):
        found = []
        for dr in (1, -1):
            for part in range(4):
                k = 4 * ((1 - dr) // 2) + part
                copy = remote(
                    source.at[pl.ds(src_rows[dr][0] + 4 * part, 4)],
                    targets[dr].at[pl.ds(4 * part, 4)],
                    send.at[k],
                    recv.at[k],
                    peer(dr, 0),
                )
                found.append((dr, copy))
        return found

    def corner_copy(packed, rims, send, recv, dr, dc):
        k = 8 + (1 - dr) + (1 - dc) // 2
        return remote(
            packed.at[(1 + dc) // 2, pl.ds(6 if dr == 1 else 0, 2)],
            rims.at[(1 - dc) // 2, pl.ds(0 if dr == 1 else 10, 2)],
            send.at[k],
            recv.at[k],
            peer(dr, dc),
        )

    def side_copy(packed, rims, send, recv, dc, chunk):
        k = 12 + 4 * ((1 - dc) // 2) + chunk
        return remote(
            packed.at[(1 + dc) // 2, pl.ds(2 * chunk, 2)],
            rims.at[(1 - dc) // 2, pl.ds(2 * chunk + 2, 2)],
            send.at[k],
            recv.at[k],
            peer(0, dc),
        )

    def when_started(dr, dc, act):
        @pl.when(exists(dr, dc))
        def _():
            act()

    def when_expected(dr, dc, act):
        @pl.when(exists(-dr, -dc))
        def _():
            act()

    early = [((dr, 0), copy) for dr, copy in row_copies(
        pre.at[1],
        {dr: pre_e.at[pl.ds(*dst_rows[dr])] for dr in (1, -1)},
        a_send,
        a_recv,
    )]
    for chunk in range(4):
        for dc in (1, -1):
            early.append(((0, dc), side_copy(pack, rim, a_send, a_recv, dc, chunk)))
    for dr in (1, -1):
        for dc in (1, -1):
            early.append(((dr, dc), corner_copy(pack, rim, a_send, a_recv, dr, dc)))
    late_rows = row_copies(
        m0_e.at[pl.ds(DMAX, rows)], {1: m0_rows.at[0], -1: m0_rows.at[1]}, m_send, m_recv
    )
    late_corners = []
    for dr in (1, -1):
        for dc in (1, -1):
            k = 16 + (1 - dr) + (1 - dc) // 2
            copy = remote(
                pack_c.at[(1 + dc) // 2, pl.ds(2 if dr == 1 else 0, 2)],
                rim_c.at[(1 - dc) // 2, pl.ds(0 if dr == 1 else 2, 2)],
                m_send.at[k],
                m_recv.at[k],
                peer(dr, dc),
            )
            late_corners.append(((dr, dc), copy))

    def late_side(chunk, dc):
        k = 8 + 4 * ((1 - dc) // 2) + chunk
        return remote(
            pack0.at[(1 + dc) // 2, pl.ds(2 * chunk, 2)],
            rim0.at[(1 + dc) // 2, pl.ds(2 * chunk, 2)],
            m_send.at[k],
            m_recv.at[k],
            peer(0, dc),
        )

    lane = lax.broadcasted_iota(jnp.int32, (DMAX, cols), 1).astype(F32).astype(BF)
    lane = jnp.concatenate([lane] * (chans // DMAX), axis=0)
    lane_e = lax.broadcasted_iota(jnp.int32, (ext, cols), 1)
    lane_b = lax.broadcasted_iota(jnp.int32, (8, cols), 1)

    def picks(size, *wanted):
        k = lax.broadcasted_iota(jnp.int32, (size, wanted[0].shape[1]), 0)
        found = k == wanted[0]
        for other in wanted[1:]:
            found = found | (k == other)
        return jnp.where(found, 1.0, 0.0).astype(BF)

    n_wide = lax.broadcasted_iota(jnp.int32, (1, 2 * cols), 1)
    n_one = lax.broadcasted_iota(jnp.int32, (1, cols), 1)
    w_wide = jnp.where(n_wide < cols, n_wide, n_wide - cols)
    group = w_wide // 16
    inner = w_wide % 16
    pmat[...] = picks(
        8 * cols,
        jnp.where(
            n_wide < cols,
            group * cols + inner,
            ((group + 1) % 8) * cols + cols - DMAX + inner,
        ),
    )

    def pack_rows(values):
        both = jnp.dot(
            jnp.concatenate(values, axis=1), pmat[...], preferred_element_type=F32
        ).astype(BF)
        return both[:, 0:cols], both[:, cols:]

    def send_outer(which):
        for dr, copy in late_rows:
            if dr == which:
                when_started(dr, 0, copy.start)
        for half in (0, 1):
            g = half + (6 if which == 1 else 0)
            left, right = pack_rows([m0_e[DMAX + 8 * g + i] for i in range(8)])
            slot = half + (2 if which == 1 else 0)
            pack_c[0, slot] = left
            pack_c[1, slot] = right
        for (dr, dc), copy in late_corners:
            if dr == which:
                when_started(dr, dc, copy.start)

    def merged(rims, g, i):
        return jnp.where((lane >= 16 * i) & (lane < 16 * i + 16), rims[1, g], rims[0, g])

    d1 = dil[1]
    d0 = dil[0]

    def side_shift(tile, halo, index, d):
        where, split = lane_e, d if index == 0 else cols - d
        if index == 0:
            return pltpu.roll(jnp.where(where >= split, tile, halo), cols - d, 1)
        return pltpu.roll(jnp.where(where < split, tile, halo), d, 1)

    loads[0].wait()

    @pl.loop(0, 4)
    def _(chunk):
        for half in (0, 1):
            g = 2 * chunk + half
            left, right = pack_rows([pre_e[DMAX + 8 * g + i] for i in range(8)])
            pack[0, g] = left
            pack[1, g] = right

    pl.semaphore_wait(barrier, expected)
    for (dr, dc), copy in early:
        when_started(dr, dc, copy.start)

    loads[1].wait()
    loads[2].wait()
    own = jnp.where(occ[...] > 0, cot[...].astype(F32), 0.0).astype(BF)
    s_own[...] = own
    s_in[1, pl.ds(DMAX, rows)] = own
    s_copies = []
    for k, (dr, dc) in enumerate(AROUND):
        copy = remote(
            s_own.at[pl.ds(*src_rows[dr])],
            s_in.at[1 - dc, pl.ds(*dst_rows[dr])],
            s_send.at[k],
            s_recv.at[k],
            peer(dr, dc),
        )
        s_copies.append(((dr, dc), copy))
        when_started(dr, dc, copy.start)

    loads[3].wait()
    loads[4].wait()
    eye = jnp.where(
        lax.broadcasted_iota(jnp.int32, (chans, chans), 0)
        == lax.broadcasted_iota(jnp.int32, (chans, chans), 1),
        1.0,
        0.0,
    ).astype(F32)
    eye_b = eye.astype(BF)

    def tap(t):
        return w[0, pl.ds(t * chans, chans), :]

    def turned(value):
        return lax.dot_general(eye_b, value, NT, preferred_element_type=F32).astype(BF)

    w1l[...] = turned(w[1])
    c0row = coup[0:1, :].astype(F32)
    c1row = coup[1:2, :].astype(F32)
    c0col = jnp.dot(
        (eye * c0row).astype(BF), jnp.ones((chans, cols), BF), preferred_element_type=F32
    )
    c0col_b = c0col.astype(BF)
    c1rows = jnp.broadcast_to(c1row, (8, chans))
    diag = (
        lax.broadcasted_iota(jnp.int32, (8, 8 * chans), 1) // chans
        == lax.broadcasted_iota(jnp.int32, (8, 8 * chans), 0)
    )
    heads = lax.dot_general(
        c1rows.astype(BF), w[0], NT, preferred_element_type=F32
    )
    def make_shifts(layer, d):
        right = n_wide + d
        left = w_wide - d
        for i in range(8):
            smat[layer, i] = picks(
                2 * cols,
                jnp.where(
                    n_wide < cols,
                    jnp.where(right < cols, right, right + 16 * i),
                    jnp.where(left >= 0, left, cols + ((left + 16 * i + cols) % cols)),
                ),
            )
    make_shifts(1, d1)

    def prepare_last():
        for b in range(3):
            w0o[pl.ds(b * chans, chans), :] = turned(
                jnp.concatenate([tap(3 * a + b) for a in range(3)], axis=0)
            )

        make_shifts(0, d0)
        for i in range(8):
            umat[i] = picks(
                cols,
                jnp.where(
                    n_one < DMAX,
                    n_one + 16 * i,
                    jnp.where(n_one >= cols - DMAX, (n_one + 16 * i) % cols, -1),
                ),
            )
        omat[...] = picks(
            2 * cols,
            jnp.where(
                n_wide < cols,
                jnp.where(w_wide + d0 < cols, w_wide + d0, -1),
                jnp.where(w_wide >= cols - d0, w_wide + d0 - cols, -1),
            ),
            jnp.where(
                n_wide < cols,
                jnp.where(w_wide >= d0, cols + w_wide - d0, -1),
                jnp.where(w_wide < d0, 2 * cols + w_wide - d0, -1),
            ),
        )
        w0r[0] = turned(w[0, pl.ds(6 * chans, 3 * chans), :])
        w0r[1] = turned(w[0, pl.ds(0, 3 * chans), :])
        for side in (0, 1):
            m0_e[pl.ds(side * (DMAX + rows), DMAX)] = jnp.zeros((DMAX, chans, cols), BF)
            outside[side, pl.ds(16 - 16 * side, 16)] = jnp.zeros((DMAX, 3 * chans, cols), BF)

    def spread(value):
        return jnp.where(diag, jnp.concatenate([value] * 8, axis=1), 0.0)

    vb[...] = jnp.concatenate(
        [spread(heads[:, t * chans : (t + 1) * chans]) for t in range(9)], axis=0
    ).astype(BF)
    cb[...] = jnp.concatenate([spread(c1rows)] * 2, axis=0).astype(BF)
    for t in range(9):
        for start in (DMAX, 2 * DMAX + rows):
            pmap[t, pl.ds(start, DMAX), :] = jnp.zeros((DMAX, cols), F32)
            pmap[t, pl.ds(start - DMAX if start == DMAX else start + DMAX, DMAX), :] = (
                jnp.zeros((DMAX, cols), F32)
            )
    for start in (0, DMAX + rows):
        cmap[pl.ds(start, DMAX), :] = jnp.zeros((DMAX, cols), F32)

    for (dr, dc), copy in early:
        when_expected(dr, dc, copy.wait_recv)

    @pl.loop(0, 3)
    def _(part):
        for i in range(8):
            wide_in = []
            for quarter in range(4):
                g = part * 4 + quarter
                e = g * 8 + i
                tile = jnp.where(pre_e[e] > 0, c0col_b, 0)
                halo = jnp.where(merged(rim, g, i) > 0, c0col_b, 0)
                shifted[e, pl.ds(chans, chans), :] = tile
                wide_in.append(jnp.concatenate([tile, halo], axis=1))
            both = jnp.dot(
                jnp.concatenate(wide_in, axis=0), smat[1, i], preferred_element_type=F32
            ).astype(BF)
            for quarter in range(4):
                e = (part * 4 + quarter) * 8 + i
                here = both[quarter * chans : (quarter + 1) * chans]
                shifted[e, pl.ds(0, chans), :] = here[:, 0:cols]
                shifted[e, pl.ds(2 * chans, chans), :] = here[:, cols:]

    loads[5].wait()

    middle = (level > 0) & (level + 2 < n_level)
    direct = level + 2 >= n_level

    @pl.when(middle)
    def _():
        for t in range(9):
            w1t[t] = turned(w[1, pl.ds(t * chans, chans), :])

        @pl.loop(0, 4)
        def _(chunk):
            keep = [pre0[chunk * 16 + i] > 0 for i in range(16)]
            for t in range(10):
                if t < 9:
                    taps_in = jnp.concatenate(
                        [
                            shifted[
                                chunk * 16 + i + DMAX - (t // 3 - 1) * d1,
                                pl.ds((t % 3) * chans, chans),
                                :,
                            ]
                            for i in range(16)
                        ],
                        axis=1,
                    )
                    made = jnp.dot(w1t[t], taps_in, preferred_element_type=F32).astype(BF)
                    pieces = [made[:, i * cols : (i + 1) * cols] for i in range(16)]
                else:
                    pieces = [c0col_b] * 16
                kept = [jnp.where(keep[i], pieces[i], 0) for i in range(16)]
                for target, lhs, values in ((tmap, vb, kept), (tcen, cb, pieces)):
                    rhs = jnp.concatenate(
                        [
                            jnp.concatenate(values[0:8], axis=0),
                            jnp.concatenate(values[8:16], axis=0),
                        ],
                        axis=1,
                    )
                    maps = jnp.dot(lhs[...], rhs, preferred_element_type=F32)
                    size = target.shape[2]
                    target[t, 2 * chunk] = maps[0:size, 0:cols]
                    target[t, 2 * chunk + 1] = maps[0:size, cols : 2 * cols]

    for (dr, dc), copy in s_copies:
        when_expected(dr, dc, copy.wait_recv)

    q_copies = []
    for k, (dr, dc) in enumerate(NINE):
        if dc == 0:
            src = q_msg.at[pl.ds(*{1: (80, 48), 0: (16, 128), -1: (0, 48)}[dr])]
            dst = in_tile if dr == 0 else in_row.at[(1 - dr) // 2]
        elif dr == 0:
            src = q_side.at[(1 - dc) // 2]
            dst = in_side.at[(1 - dc) // 2]
        else:
            src = q_side.at[(1 - dc) // 2, pl.ds(0, 16)]
            dst = in_corner.at[(1 - dc) // 2, (1 - dr) // 2]
        q_copies.append(((dr, dc), remote(src, dst, q_send.at[k], q_recv.at[k], peer(dr, dc, -1))))

    @pl.when(level + 1 < n_level)
    def _():
        prepare_last()

    for (dr, dc), copy in q_copies:

        @pl.when(exists(-dr, -dc) & (level + 1 < n_level))
        def _():
            copy.wait_recv()

    low = lane_e < DMAX
    high = lane_e >= cols - DMAX

    def folded(value):
        found = []
        for j in (0, 2, 1):
            block = value[32 * j : 32 * j + 8]
            block = pltpu.roll(block, DMAX, 1)
            for m in range(1, 4):
                start = 32 * j + 8 * m
                piece = pltpu.roll(value[start : start + 8], (DMAX + 32 * m) % cols, 1)
                block = jnp.where(lane_b // 32 == m, piece, block)
            found.append(block)
        found.append(jnp.zeros((8, cols), F32))
        return jnp.concatenate(found, axis=0).astype(BF)

    def unfolded(block):
        return jnp.concatenate(
            [pltpu.roll(block, (cols - DMAX - 32 * m) % cols, 1) for m in range(4)], axis=0
        )

    def summed(middle, above, below):
        middle, above, below = (part.astype(F32) for part in (middle, above, below))
        return jnp.concatenate(
            [
                unfolded(middle[0:8]) + unfolded(above[8:16]),
                unfolded(middle[16:24]),
                unfolded(middle[8:16]) + unfolded(below[0:8]),
            ],
            axis=0,
        )

    left = summed(in_side[0], in_corner[0, 0], in_corner[0, 1])
    right = summed(in_side[1], in_corner[1, 0], in_corner[1, 1])
    edges = jnp.concatenate(
        [
            in_row[0, pl.ds(0, 32)].astype(F32),
            jnp.zeros((rows - 2 * DMAX, cols), F32),
            in_row[1, pl.ds(16, 32)].astype(F32),
        ],
        axis=0,
    )
    tile = in_tile[pl.ds(0, ext)].astype(F32) + edges + s_in[1].astype(F32)
    tile += jnp.where(low, left, 0.0) + jnp.where(high, right, 0.0)
    halo = summed(in_tile[pl.ds(ext, 32)], in_row[0, pl.ds(32, 16)], in_row[1, pl.ds(0, 16)])
    halo += jnp.where(low, right + s_in[2].astype(F32), left + s_in[0].astype(F32))
    totals[0] = side_shift(tile, halo, 0, d1)
    totals[1] = tile
    totals[2] = side_shift(tile, halo, 2, d1)

    def layer_1(chunk):
        for pair in range(8):
            wide_in = []
            for i in range(2):
                r = chunk * 16 + pair * 2 + i
                parts = []
                for a in (-1, 0, 1):
                    e = r + DMAX - a * d1
                    for b in range(3):
                        line = jnp.broadcast_to(totals[b, pl.ds(e, 1), :], (16, cols)).astype(BF)
                        line = jnp.concatenate([line] * 4, axis=0)
                        parts.append(shifted[e, pl.ds(b * chans, chans), :] * line)
                wide_in.append(jnp.concatenate(parts, axis=0))
            result = jnp.dot(
                w1l[...], jnp.concatenate(wide_in, axis=1), preferred_element_type=F32
            )
            for i in range(2):
                r = chunk * 16 + pair * 2 + i
                value = result[:, i * cols : (i + 1) * cols]
                value += c0col * totals[1, pl.ds(r + DMAX, 1), :]
                grad1[r] = value
                kept = jnp.where(pre0[r] > 0, value.astype(BF), 0)
                m0_e[r + DMAX] = kept

    def prediction_maps(chunk):
        for half in range(2):
            g = chunk * 2 + half
            first = jnp.concatenate([m0_e[DMAX + g * 8 + i] for i in range(8)], axis=0)
            maps = jnp.dot(vb[...], first, preferred_element_type=F32)
            second = jnp.concatenate([grad1[g * 8 + i].astype(BF) for i in range(8)], axis=0)
            center = jnp.dot(cb[...], second, preferred_element_type=F32)
            at = pl.ds(pl.multiple_of(g * 8, 8) + 2 * DMAX, 8)
            for t in range(9):
                pmap[t, at, :] = maps[8 * t : 8 * t + 8]
            cmap[pl.ds(pl.multiple_of(g * 8, 8) + DMAX, 8), :] = center[0:8]

    def column(b):
        found = None
        for a in (-1, 0, 1):
            piece = pmap[(a + 1) * 3 + b + 1, pl.ds(DMAX - a * d0, ext), :]
            found = piece if found is None else found + piece
        return found

    @pl.when(direct)
    def _():
        @pl.loop(0, 4)
        def _(chunk):
            layer_1(chunk)
            prediction_maps(chunk)

    @pl.when(middle)
    def _():
        @pl.loop(0, 4)
        def _(chunk):
            for half in range(2):
                g = chunk * 2 + half
                lines = [
                    totals[t % 3, pl.ds(g * 8 + DMAX - (t // 3 - 1) * d1, 8), :]
                    for t in range(9)
                ]
                lines.append(totals[1, pl.ds(pl.multiple_of(g * 8, 8) + DMAX, 8), :])
                start = pl.multiple_of(g * 8, 8)
                for k in range(9):
                    found = lines[0] * tmap[0, g, pl.ds(8 * k, 8), :]
                    for t in range(1, 10):
                        found += lines[t] * tmap[t, g, pl.ds(8 * k, 8), :]
                    pmap[k, pl.ds(start + 2 * DMAX, 8), :] = found
                found = lines[0] * tcen[0, g]
                for t in range(1, 10):
                    found += lines[t] * tcen[t, g]
                cmap[pl.ds(start + DMAX, 8), :] = found

    @pl.when(level > 0)
    def _():
        goes_left = pltpu.roll(column(-1), cols - d0, 1)
        goes_right = pltpu.roll(column(1), d0, 1)
        q0 = cmap[...] + column(0)
        q0 += jnp.where(lane_e < cols - d0, goes_left, 0.0)
        q0 += jnp.where(lane_e >= d0, goes_right, 0.0)
        q1 = jnp.where(lane_e >= cols - d0, goes_left, 0.0)
        q1 += jnp.where(lane_e < d0, goes_right, 0.0)
        q_side[0] = folded(jnp.where(low, q1, q0))
        q_side[1] = folded(jnp.where(low, q0, q1))
        rim_part = folded(q1)
        q_msg[pl.ds(0, DMAX)] = rim_part[0:DMAX]
        q_msg[pl.ds(DMAX, ext)] = q0.astype(BF)
        q_msg[pl.ds(DMAX + ext, 32)] = rim_part
        for (dr, dc), copy in q_copies:
            when_started(dr, dc, copy.start)

    @pl.when(level + 1 == n_level)
    def _():
        prepare_last()

    @pl.when(level + 2 < n_level)
    def _():
        @pl.loop(0, 4)
        def _(step):
            layer_1(jnp.where(step == 0, 0, jnp.where(step == 1, 3, step - 1)))

            @pl.when(step == 0)
            def _():
                send_outer(-1)

            @pl.when(step == 1)
            def _():
                send_outer(1)

    @pl.when(direct)
    def _():
        send_outer(-1)
        send_outer(1)

    def store(chunk):
        span = pl.ds(chunk * 16, 16)
        return pltpu.make_async_copy(out_v.at[span], out.at[span], out_sem.at[chunk])

    @pl.loop(0, 4)
    def _(chunk):
        outer = []
        for pair in range(8):
            wide_in = []
            for i in range(2):
                r = chunk * 16 + pair * 2 + i
                wide_in.append(
                    jnp.concatenate([m0_e[r + DMAX - a * d0] for a in (-1, 0, 1)], axis=0)
                )
            result = jnp.dot(
                w0o[...], jnp.concatenate(wide_in, axis=1), preferred_element_type=F32
            )
            moved = jnp.dot(
                jnp.concatenate(
                    [
                        jnp.concatenate(
                            [
                                result[0:chans, i * cols : (i + 1) * cols],
                                result[2 * chans :, i * cols : (i + 1) * cols],
                            ],
                            axis=1,
                        )
                        for i in range(2)
                    ],
                    axis=0,
                ).astype(BF),
                omat[...],
                preferred_element_type=F32,
            )
            for i in range(2):
                r = chunk * 16 + pair * 2 + i
                here = moved[i * chans : (i + 1) * chans]
                outer.append(here[:, cols:].astype(BF))
                grad1[r] = (
                    grad1[r] + result[chans : 2 * chans, i * cols : (i + 1) * cols] + here[:, 0:cols]
                )
        for half in range(2):
            to_right, to_left = pack_rows(outer[8 * half : 8 * half + 8])
            pack0[0, 2 * chunk + half] = to_left
            pack0[1, 2 * chunk + half] = to_right
        for dc in (1, -1):
            when_started(0, dc, late_side(chunk, dc).start)

    def finish(chunk, more):
        for dc in (1, -1):
            when_expected(0, dc, late_side(chunk, dc).wait_recv)
        for i in range(8):
            extra = jnp.dot(
                jnp.concatenate([merged(rim0, chunk * 2 + half, i) for half in range(2)], axis=0),
                umat[i],
                preferred_element_type=F32,
            )
            for half in range(2):
                r = chunk * 16 + half * 8 + i
                value = grad1[r] + extra[half * chans : (half + 1) * chans]
                if more is not None:
                    value += more[8 * half + i]
                out_v[r] = value.astype(BF)
        store(chunk).start()

    @pl.loop(1, 3)
    def _(chunk):
        finish(chunk, None)

    for dr, copy in late_rows:
        when_expected(dr, 0, copy.wait_recv)
    for (dr, dc), copy in late_corners:
        when_expected(dr, dc, copy.wait_recv)

    @pl.loop(0, 2)
    def _(side):
        for i in range(8):
            wide_in = []
            for half in range(2):
                tile = m0_rows[side, 8 * half + i]
                halo = merged(rim_c, 2 * side + half, i)
                outside[side, 16 * side + 8 * half + i, pl.ds(chans, chans), :] = tile
                wide_in.append(jnp.concatenate([tile, halo], axis=1))
            both = jnp.dot(
                jnp.concatenate(wide_in, axis=0), smat[0, i], preferred_element_type=F32
            ).astype(BF)
            for half in range(2):
                e = 16 * side + 8 * half + i
                here = both[half * chans : (half + 1) * chans]
                outside[side, e, pl.ds(0, chans), :] = here[:, 0:cols]
                outside[side, e, pl.ds(2 * chans, chans), :] = here[:, cols:]

    @pl.loop(0, 2)
    def _(side):
        first = jnp.where(side == 0, DMAX - d0, d0)
        more = []
        for pair in range(8):
            wide_in = [outside[side, first + pair * 2 + i] for i in range(2)]
            result = jnp.dot(
                w0r[side], jnp.concatenate(wide_in, axis=1), preferred_element_type=F32
            )
            more += [result[:, i * cols : (i + 1) * cols] for i in range(2)]
        finish(3 * side, more)

    for (dr, dc), copy in early:
        when_started(dr, dc, copy.wait_send)
    for dr, copy in late_rows:
        when_started(dr, 0, copy.wait_send)
    for (dr, dc), copy in late_corners:
        when_started(dr, dc, copy.wait_send)
    for dc in (1, -1):
        for chunk in range(4):
            when_started(0, dc, late_side(chunk, dc).wait_send)
    for (dr, dc), copy in s_copies:
        when_started(dr, dc, copy.wait_send)

    @pl.when(level > 0)
    def _():
        for (dr, dc), copy in q_copies:
            when_started(dr, dc, copy.wait_send)

    for chunk in range(4):
        store(chunk).wait()


def solution(mesh):
    shape = (mesh.shape["row"], mesh.shape["col"], mesh.shape["level"])

    def on_device(pre_acts, pred_cot, occupancy, conv_weights, coupling, dilation):
        hbm = pl.BlockSpec(memory_space=pl.ANY)
        smem = pl.BlockSpec(memory_space=pltpu.SMEM)
        dma = pltpu.SemaphoreType.DMA
        result = pl.pallas_call(
            functools.partial(kernel, shape),
            out_shape=jax.ShapeDtypeStruct((64, 64, 128), BF),
            in_specs=[smem, hbm, hbm, hbm, hbm, hbm],
            out_specs=hbm,
            scratch_shapes=[
                pltpu.VMEM((64, 128), BF),
                pltpu.VMEM((64, 128), jnp.int32),
                pltpu.VMEM((2, 576, 64), BF),
                pltpu.VMEM((2, 64), BF),
                pltpu.VMEM((96, 64, 128), BF),
                pltpu.VMEM((64, 64, 128), BF),
                pltpu.VMEM((2, 8, 64, 128), BF),
                pltpu.VMEM((2, 12, 64, 128), BF),
                pltpu.VMEM((64, 128), BF),
                pltpu.VMEM((3, 96, 128), BF),
                pltpu.VMEM((96, 192, 128), BF),
                pltpu.VMEM((96, 64, 128), BF),
                pltpu.VMEM((2, 16, 64, 128), BF),
                pltpu.VMEM((2, 4, 64, 128), BF),
                pltpu.VMEM((2, 4, 64, 128), BF),
                pltpu.VMEM((2, 32, 192, 128), BF),
                pltpu.VMEM((2, 8, 64, 128), BF),
                pltpu.VMEM((2, 8, 64, 128), BF),
                pltpu.VMEM((64, 64, 128), F32),
                pltpu.VMEM((3, 96, 128), F32),
                pltpu.VMEM((9, 128, 128), F32),
                pltpu.VMEM((96, 128), F32),
                pltpu.VMEM((144, 128), BF),
                pltpu.VMEM((2, 32, 128), BF),
                pltpu.VMEM((128, 128), BF),
                pltpu.VMEM((2, 32, 128), BF),
                pltpu.VMEM((2, 48, 128), BF),
                pltpu.VMEM((2, 2, 16, 128), BF),
                pltpu.VMEM((64, 576), BF),
                pltpu.VMEM((9, 64, 64), BF),
                pltpu.VMEM((10, 8, 72, 128), F32),
                pltpu.VMEM((10, 8, 8, 128), F32),
                pltpu.VMEM((192, 192), BF),
                pltpu.VMEM((2, 64, 192), BF),
                pltpu.VMEM((1024, 256), BF),
                pltpu.VMEM((2, 8, 256, 256), BF),
                pltpu.VMEM((8, 128, 128), BF),
                pltpu.VMEM((256, 256), BF),
                pltpu.VMEM((72, 512), BF),
                pltpu.VMEM((16, 512), BF),
                pltpu.VMEM((64, 64, 128), BF),
                dma((6,)),
                dma((4,)),
                dma((20,)),
                dma((20,)),
                dma((8,)),
                dma((8,)),
                dma((9,)),
                dma((9,)),
                dma((20,)),
                dma((20,)),
            ],
            compiler_params=pltpu.CompilerParams(
                collective_id=0, has_side_effects=True, vmem_limit_bytes=64 * 2**20
            ),
        )(
            dilation,
            pre_acts.reshape(2, 64, 64, 128),
            pred_cot.reshape(64, 128),
            occupancy.reshape(64, 128),
            conv_weights.reshape(2, 576, 64),
            coupling.reshape(2, 64),
        )
        return result[None]

    return jax.shard_map(
        on_device,
        mesh=mesh,
        in_specs=(
            P("level", None, "row", None, "col"),
            P("level", "row", "col"),
            P("level", "row", "col"),
            P("level", None, None, None, None, None),
            P("level", None, None),
            P(),
        ),
        out_specs=P("level", "row", None, "col"),
        check_vma=False,
    )
```
